32 devices in a mesh: runs: 2 (over y), space: 4 (over z), spec: 4 (over x, core).
Axes of the slice: x: 2, y: 2, z: 4, core: 2. Of those that a mesh axis runs over, the one named last changes fastest.
Arguments:
- spectrum: float32 [36, 36, 1024], P('spec', None, ('runs', 'space')), parts along dimension 2, may hold values from 0.012 to 6.01, as said below
- courant: float32 [36, 36, 512], P('spec', None, 'space'), may hold values from 0.1 to 0.9
- refraction: float32 [36, 36, 512], P('spec', None, 'space'), may hold values from -0.4 to 0.4
- growth: float32 [36, 1024], P(None, ('runs', 'space')), parts along dimension 1, may hold values from 0 to 0.5
- dissip: float32 [36], replicated, may hold values from 0.5 to 2
- upwind: int32 [36, 512], P('spec', 'space'), may hold values from 0 to 511, as said below
- send_order: int32 [512], P('space'), may hold values from 0 to 511, as said below
Outputs:
- energy_out: float32 [36, 36, 1024], P('spec', None, ('runs', 'space')), parts along dimension 2
- series: float32 [12, 1024], P(None, ('runs', 'space')), parts along dimension 1
The draws below stay inside these ranges and needn't reach their ends.
There are 2 independent parts, one for each index of `runs`. The reference program is written for one: setup_inputs(seed, part) draws one part's arguments, and reference() takes and returns one part's arrays. A program takes and returns all parts, laid end to end along the dimension named above; an argument that names none is the same for every part. Nothing has to cross between parts.
Inputs may be any that keep to these rules, and one draw needn't show every extreme that they name: Each point and its upwind point lie within 16 positions of each other in the cyclic order of points; offsets of exactly 16 and - 16 occur. `send_order`: entries s * 128 to (s + 1) * 128 - 1 are a permutation of the points of tile s. `spectrum`: positive energies.
All inputs are finite; a program needn't handle non-finite values.
Results may differ from the reference program's by a relative error of at most 0.0001.
Values sent between devices are 32-bit elements; how exact they have to be, the bound alone decides.
No kernel may reach another device: no remote copies, remote signals or barrier semaphores. Data moves between devices by JAX's collectives and lax.ppermute only.
A program may use at most 64 MiB of HBM per device.

```python
import math
import jax
import jax.numpy as jnp
from jax import lax

ND = 36
NF = 36
PT_DEV = 128
STEPS = 6
REACH = 16
POINTS = 512
N_SPACE = 4


def draw_spectrum(key, part):
    direc = jnp.arange(ND, dtype=jnp.float32)[:, None, None]
    fidx = jnp.arange(NF, dtype=jnp.float32)[None, :, None]
    shape_factor = 3.0 ** (direc / (ND - 1)) * 4.0 ** (-fidx / (NF - 1))
    base = jnp.exp(jax.random.uniform(key, (ND, NF, POINTS), jnp.float32, math.log(0.05), math.log(2.0)))
    return (base * shape_factor).astype(jnp.float32)


def draw_upwind(key, part):
    offsets = jax.random.randint(key, (ND, POINTS), -REACH, REACH + 1)
    offsets = offsets.at[0, 0].set(-1).at[0, 1].set(-1).at[0, 2].set(REACH).at[0, 3].set(-REACH)
    base = jnp.arange(POINTS, dtype=jnp.int32)[None, :]
    return jnp.mod(base + offsets, POINTS).astype(jnp.int32)


def draw_send_order(key, part):
    tiles = POINTS // PT_DEV
    keys = jax.random.split(key, tiles)
    orders = jax.vmap(lambda single: jax.random.permutation(single, PT_DEV))(keys)
    offsets = PT_DEV * jnp.arange(tiles, dtype=jnp.int32)[:, None]
    return (orders.astype(jnp.int32) + offsets).reshape(POINTS).astype(jnp.int32)


def block_scale(stream_key, shape, pieces, smallest, top_value):
    level, own = 1.0, jax.random.fold_in(stream_key, 6)
    for axis_at, shards_of in pieces:
        heights = jnp.exp(jax.random.uniform(jax.random.fold_in(own, axis_at), (shards_of,), jnp.float32, smallest / len(pieces), top_value / len(pieces)))
        level = level * jnp.repeat(heights, shape[axis_at] // shards_of).reshape([-1 if axis == axis_at else 1 for axis in range(len(shape))])
    return level


def setup_inputs(seed: int = 0, part: int = 0) -> dict:
    splits = jax.random.split(jax.random.key(seed), 8)
    own_keys = jax.random.split(jax.random.fold_in(splits[7], part), 8)
    return {
        "spectrum": draw_spectrum(jax.random.fold_in(jax.random.fold_in(splits[7], part), 71), part),
        "courant": jnp.clip(0.1 + 0.79999997 * jax.random.uniform(splits[1], (ND, NF, POINTS), jnp.float32) ** block_scale(splits[1], (ND, NF, POINTS), ((0, 4), (2, 4)), -0.2, 0.2), 0.1, 0.9),
        "refraction": jnp.clip(jax.random.uniform(splits[2], (ND, NF, POINTS), jnp.float32, -0.4, 0.4) * block_scale(splits[2], (ND, NF, POINTS), ((0, 4), (2, 4)), -0.4, 0.0), -0.4, 0.4),
        "growth": jnp.clip(0.5 * jax.random.uniform(own_keys[3], (NF, POINTS), jnp.float32) ** block_scale(own_keys[3], (NF, POINTS), ((1, 4),), -0.2, 0.2), 0.0, 0.5),
        "dissip": jnp.clip(jnp.exp(jax.random.uniform(splits[4], (NF,), jnp.float32, math.log(0.5), math.log(2.0))), 0.5, 2.0),
        "upwind": draw_upwind(jax.random.fold_in(splits[7], 71), part),
        "send_order": draw_send_order(jax.random.fold_in(splits[7], 71), part),
    }


def frequency_table(count):
    return 0.035 * jnp.float32(1.1) ** jnp.arange(count, dtype=jnp.float32)

def reference(spectrum, courant, refraction, growth, dissip, upwind, send_order):
    freqs = frequency_table(NF)
    energy = spectrum
    bins = ND * NF
    fields = []
    for hour in range(STEPS):
        upstream = jax.vmap(lambda block, index: jnp.take(block, index, axis=1))(energy, upwind)
        moved = energy + courant * (upstream - energy)
        flux = jnp.maximum(refraction, 0.0) * moved + jnp.minimum(refraction, 0.0) * jnp.roll(moved, -1, axis=0)
        turned = moved - flux + jnp.roll(flux, 1, axis=0)
        mean_energy = lax.optimization_barrier(jnp.sum(turned, axis=(0, 1))) / bins
        energy = turned * (1.0 + growth)[None] / (1.0 + dissip[:, None] * mean_energy[None, :])[None]
        zeroth = lax.optimization_barrier(jnp.sum(energy, axis=(0, 1)))
        first = lax.optimization_barrier(jnp.sum(energy * freqs[None, :, None], axis=(0, 1)))
        fields.append(jnp.stack([4.0 * jnp.sqrt(zeroth / bins), zeroth / first]))
    stacked = jnp.stack(fields).transpose(1, 0, 2).reshape(2 * STEPS, POINTS)
    share = PT_DEV // N_SPACE
    order = send_order.reshape(N_SPACE, N_SPACE, share).transpose(1, 0, 2).reshape(POINTS)
    series = jnp.take(stacked, order, axis=1)
    return (energy, series)
```

```python
import functools

import jax
import jax.numpy as jnp
from jax import lax
from jax.experimental import pallas as pl
from jax.experimental.pallas import tpu as pltpu
from jax.sharding import PartitionSpec as P

STEPS = 6
ROWS = 40
F32 = jnp.float32


def frequency_table(count):
    return 0.035 * jnp.float32(1.1) ** jnp.arange(count, dtype=jnp.float32)


def subtile_of(s, k, n):
    return jnp.where(s % 2 == 0, k, n - 1 - k)


def far_route(tiles, n):
    route = []
    for s in range(tiles):
        for k in range(n):
            q = k if s % 2 == 0 else n - 1 - k
            at = s * n + q
            to = (at - 1 if q % 2 == 0 else at + 1) % (tiles * n)
            ts, tq = divmod(to, n)
            route.append((s * n + k, ts * n + (tq if ts % 2 == 0 else n - 1 - tq)))
    return route


def lanes(shape):
    return lax.broadcasted_iota(jnp.int32, shape, len(shape) - 1)


class Spot:
    def __init__(self, n, npt):
        self.n, self.sub, self.npt = n, npt // n, npt
        self.s, self.k = lax.axis_index("space"), lax.axis_index("spec")
        self.q = subtile_of(self.s, self.k, n)
        self.qn = self.q ^ 1
        self.qf = n - 1 - self.q
        self.even = self.q % 2 == 0

    def shift(self, to, frm):
        return ((to - frm + self.n) % self.n) * self.sub

    def block(self, shape):
        return lanes(shape) // self.sub


def move(x, amount):
    return pltpu.roll(x, amount, 1)


def offsets(upwind, s, npt, total, reach):
    own = s * npt + lanes(upwind.shape)
    return (jnp.mod(upwind - own + reach, total) - reach).astype(F32)


def pack_kernel(n, total, reach, e_ref, c_ref, r_ref, u_ref, *rest):
    outs, v = rest[: n - 1], rest[n - 1]
    dirs, nfreq, npt = e_ref.shape
    at = Spot(n, npt)
    off = offsets(u_ref[...], at.s, npt, total, reach)
    for a, ref in enumerate((e_ref, c_ref, r_ref)):
        for j in range(dirs):
            v[a * dirs + j, :nfreq, :] = ref[j]
            v[a * dirs + j, nfreq:, :] = (
                jnp.broadcast_to(off[j : j + 1], (ROWS - nfreq, npt)) if a == 0 else jnp.zeros((ROWS - nfreq, npt), F32)
            )
    block = at.block((ROWS, npt))
    for d in range(1, n):
        to = subtile_of(at.s, at.k ^ d, n)
        for g in range(outs[0].shape[0]):
            row = None
            for i in range(n):
                if n * g + i >= 3 * dirs:
                    continue
                piece = move(v[n * g + i], at.shift(i, to))
                row = piece if row is None else jnp.where(block == i, piece, row)
            outs[d - 1][g] = row


def half_mask(at, shape, q, first):
    lane = lanes(shape)
    start = q * at.sub + jnp.where(first, 0, at.sub // 2)
    return (lane >= start) & (lane < start + at.sub // 2)


def packed(at, pieces, block):
    row = None
    for i, piece in enumerate(pieces):
        piece = move(piece, at.shift(i, at.q))
        row = piece if row is None else jnp.where(block == i, piece, row)
    return row


def spread_kernel(n, total, reach, e_ref, c_ref, r_ref, u_ref, g_ref, *rest):
    msgs = rest[: n - 1]
    eo, co, ro, near, far = rest[n - 1 :]
    dirs, nfreq, npt = e_ref.shape
    at = Spot(n, npt)
    off = offsets(u_ref[...], at.s, npt, total, reach)
    for out, ref in ((eo, e_ref), (co, c_ref), (ro, r_ref)):
        for j in range(dirs):
            out[dirs * at.k + j, :nfreq, :] = ref[j]
            out[dirs * at.k + j, nfreq:, :] = jnp.broadcast_to(off[j : j + 1], (ROWS - nfreq, npt))
    for d in range(1, n):
        b = at.k ^ d
        for a, out in enumerate((eo, co, ro)):
            for j in range(dirs):
                p = a * dirs + j
                out[dirs * b + j] = move(msgs[d - 1][p // n], at.shift(at.q, p % n))
    shape = (ROWS, npt)
    block = at.block(shape)
    half = at.sub // 2
    groups = n * dirs // n
    masks = {}
    for name, first in (("near", jnp.logical_not(at.even)), ("far", at.even)):
        masks[name] = (half_mask(at, shape, at.q, first), jnp.where(first, half, npt - half))
    for g in range(groups):
        row = packed(at, [eo[n * g + i] for i in range(n)], block)
        near[g] = row
        far[g] = row
        for name, out in (("near", near), ("far", far)):
            mask, amount = masks[name]
            out[groups + g] = packed(
                at, [jnp.where(mask, co[n * g + i], move(ro[n * g + i], amount)) for i in range(n)], block
            )
    far[2 * groups, :nfreq, :] = g_ref[...]
    far[2 * groups, nfreq:, :] = jnp.zeros((ROWS - nfreq, npt), F32)


def window(at, e, near, far, ew, ndir, block):
    def slab(g, _):
        for i in range(at.n):
            d = at.n * g + i
            x = jnp.where(block == at.qn, move(near[g], at.shift(at.qn, i)), e[d])
            ew[d] = jnp.where(block == at.qf, move(far[g], at.shift(at.qf, i)), x)
        return 0

    lax.fori_loop(0, ndir // at.n, slab, 0)


def hour(e, c, r, idx, out, m0s, grow1, dissip, freqs, bins, nfreq, factor):
    ndir, rows, npt = e.shape

    def moved(d):
        x = e[d]
        if factor is not None:
            x = x * factor
        index = jnp.broadcast_to(idx[pl.ds(d, 1), :], (rows, npt))
        up = jnp.take_along_axis(x, index, axis=1)
        return x + c[d] * (up - x)

    def flux(d, here, there):
        rate = r[d]
        return jnp.maximum(rate, 0.0) * here + jnp.minimum(rate, 0.0) * there

    first = moved(0)
    m0s[...] = first
    last = moved(ndir - 1)

    def body(d, carry):
        here, before, total = carry
        there = moved(d + 1)
        f = flux(d, here, there)
        turned = here - f + before
        out[d] = turned
        return there, f, total + turned

    here, before, total = lax.fori_loop(
        0, ndir - 1, body, (first, flux(ndir - 1, last, first), jnp.zeros((rows, npt), F32)), unroll=5
    )
    f = flux(ndir - 1, here, m0s[...])
    turned = here - f + before
    out[ndir - 1] = turned
    total = total + turned
    live = lax.broadcasted_iota(jnp.int32, (rows, npt), 0) < nfreq
    total = jnp.where(live, total, 0.0)
    mean = jnp.sum(total, axis=0, keepdims=True) / bins
    factor = grow1 / (1.0 + dissip * mean)
    part = jnp.where(live, factor * total, 0.0)
    zeroth = jnp.sum(part, axis=0, keepdims=True)
    first_moment = jnp.sum(part * freqs, axis=0, keepdims=True)
    return factor, 4.0 * jnp.sqrt(zeroth / bins), zeroth / first_moment


def phase_kernel(n, stage, bins, nfreq, fields_before, *refs):
    refs = list(refs)
    take = lambda count: [refs.pop(0) for _ in range(count)]
    e, near, far, dissip_ref, freqs_ref = take(5)
    if stage == 0:
        ci, ri, g_ref = take(3)
    else:
        cw, rw, idx, gw = take(4)
        old = take(fields_before)
    if stage == 0:
        cw, rw, idx, gw = take(4)
    fields = take(1)[0]
    if stage < 2:
        eo, msg = take(2)
    else:
        eo = take(1)[0]
        backs = take(n - 1)
    ew, et, m0s = take(3)
    ndir, rows, npt = e.shape
    at = Spot(n, npt)
    shape = (rows, npt)
    block = at.block(shape)
    groups = ndir // n
    window(at, e, near, far, ew, ndir, block)
    if stage == 0:
        half = at.sub // 2
        nfirst, ffirst = at.even, jnp.logical_not(at.even)
        nmask, fmask = half_mask(at, shape, at.qn, nfirst), half_mask(at, shape, at.qf, ffirst)
        nback, fback = jnp.where(nfirst, npt - half, half), jnp.where(ffirst, npt - half, half)

        def slab(g, _):
            for i in range(n):
                d = n * g + i
                pn = move(near[groups + g], at.shift(at.qn, i))
                pf = move(far[groups + g], at.shift(at.qf, i))
                cw[d] = jnp.where(nmask, pn, jnp.where(fmask, pf, ci[d]))
                rw[d] = jnp.where(nmask, move(pn, nback), jnp.where(fmask, move(pf, fback), ri[d]))
                idx[pl.ds(d, 1), :] = (lanes((1, npt)) + ew[d, nfreq : nfreq + 1, :].astype(jnp.int32)) & (npt - 1)
            return 0

        lax.fori_loop(0, groups, slab, 0)
        gw[:nfreq, :] = 1.0 + jnp.where(block[:nfreq] == at.qf, far[2 * groups, :nfreq, :], g_ref[...])
        gw[nfreq:, :] = jnp.ones((rows - nfreq, npt), F32)
    grow1, dissip, freqs = gw[...], dissip_ref[...], freqs_ref[...]
    fa, ha, pa = hour(ew, cw, rw, idx, et, m0s, grow1, dissip, freqs, bins, nfreq, None)
    fb, hb, pb = hour(et, cw, rw, idx, ew, m0s, grow1, dissip, freqs, bins, nfreq, fa)
    if stage < 2:
        fields[...] = jnp.concatenate([ha, hb, pa, pb], axis=0)

        def slab(g, _):
            row = None
            for i in range(n):
                x = ew[n * g + i] * fb
                eo[n * g + i] = x
                piece = move(x, at.shift(i, at.q))
                row = piece if row is None else jnp.where(block == i, piece, row)
            msg[g] = row
            return 0

        lax.fori_loop(0, groups, slab, 0)
    else:
        dirs = ndir // n
        h = [o[:2] for o in old] + [ha, hb]
        p = [o[2:] for o in old] + [pa, pb]
        every = jnp.concatenate(h + p + [jnp.zeros((16 - 2 * STEPS, npt), F32)], axis=0)
        fields[...] = every
        for j in range(dirs):
            eo[j] = ew[dirs * at.k + j] * fb
        m0s[...] = jnp.zeros(shape, F32)
        m0s[:16, :] = every
        tail = m0s[...]
        for d in range(1, n):
            b = at.k ^ d
            for g in range(backs[0].shape[0]):
                row = None
                for i in range(n):
                    j = n * g + i
                    if j > dirs:
                        continue
                    x = ew[dirs * b + j] * fb if j < dirs else tail
                    piece = move(x, at.shift(i, at.q))
                    row = piece if row is None else jnp.where(block == i, piece, row)
                backs[d - 1][g] = row


def join_kernel(n, nfreq, e_ref, f_ref, order_ref, *rest):
    msgs = rest[: n - 1]
    out, series = rest[n - 1 :]
    dirs, rows, npt = e_ref.shape
    at = Spot(n, npt)
    shape = (rows, npt)
    block = at.block(shape)
    fields = f_ref[...]
    qs = [subtile_of(at.s, at.k ^ d, n) for d in range(1, n)]
    for j in range(dirs + 1):
        x = e_ref[j] if j < dirs else None
        for d in range(1, n):
            piece = move(msgs[d - 1][j // n], at.shift(qs[d - 1], j % n))
            if j < dirs:
                x = jnp.where(block == qs[d - 1], piece, x)
            else:
                fields = jnp.where(block[:16] == qs[d - 1], piece[:16], fields)
        if j < dirs:
            out[j] = x[:nfreq]
    index = jnp.broadcast_to((order_ref[...] - at.s * npt).reshape(1, npt), (16, npt))
    series[...] = jnp.take_along_axis(fields, index, axis=1)


def hand_kernel(tiles, own_ref, *rest):
    others, out = rest[:-1], rest[-1]
    rows, npt = out.shape
    share = npt // tiles
    s = lax.axis_index("space")
    block = lanes((16, npt)) // share
    x = own_ref[...]
    for d in range(1, tiles):
        frm = (s - d + tiles) % tiles
        piece = move(others[d - 1][...], ((frm - s + tiles) % tiles) * share)
        x = jnp.where(block == frm, piece, x)
    out[...] = x[:rows]


def call(kernel, outs, scratch, *args):
    vm = pl.BlockSpec(memory_space=pltpu.VMEM)
    return pl.pallas_call(
        kernel,
        out_shape=[jax.ShapeDtypeStruct(shape, dtype) for shape, dtype in outs],
        in_specs=[vm] * len(args),
        out_specs=[vm] * len(outs),
        scratch_shapes=[pltpu.VMEM(shape, F32) for shape in scratch],
        compiler_params=pltpu.CompilerParams(vmem_limit_bytes=40 * 2**20),
    )(*args)


def on_device(spectrum, courant, refraction, growth, dissip, upwind, send_order):
    dirs, nfreq, npt = spectrum.shape
    tiles, n = lax.axis_size("space"), lax.axis_size("spec")
    total, reach = npt * tiles, npt // 8
    ndir = dirs * n
    bins = ndir * nfreq
    groups = ndir // n
    peers = range(1, n)
    swap = lambda x, d: lax.ppermute(x, "spec", [(k, k ^ d) for k in range(n)])
    near_to = lambda x: swap(x, 1)
    route = far_route(tiles, n)
    far_to = lambda x: lax.ppermute(x, ("space", "spec"), route)
    wide = lambda v: jnp.pad(jnp.broadcast_to(v[:, None], (nfreq, npt)), ((0, ROWS - nfreq), (0, 0)))
    freqs, dissip = wide(frequency_table(nfreq)), wide(dissip)
    field = (ROWS, npt)
    state = ((ndir, *field), F32)

    slabs = -(-3 * dirs // n)
    sent = call(
        functools.partial(pack_kernel, n, total, reach),
        [((slabs, *field), F32)] * (n - 1),
        [(3 * dirs, *field)],
        spectrum, courant, refraction, upwind,
    )
    got = [swap(x, d) for d, x in zip(peers, sent)]
    e, c, r, near, far = call(
        functools.partial(spread_kernel, n, total, reach),
        [state] * 3 + [((2 * groups, *field), F32), ((2 * groups + 1, *field), F32)],
        [],
        spectrum, courant, refraction, upwind, growth, *got,
    )
    scratch = [(ndir, *field), (ndir, *field), field]
    phase = lambda stage, before, outs, *args: call(
        functools.partial(phase_kernel, n, stage, bins, nfreq, before), outs, scratch, *args
    )
    c, r, idx, gw, f0, e, msg = phase(
        0, 0,
        [state, state, ((ndir + (-ndir) % 8, npt), jnp.int32), (field, F32), ((4, npt), F32), state, ((groups, *field), F32)],
        e, near_to(near), far_to(far), dissip, freqs, c, r, growth,
    )
    f1, e, msg = phase(
        1, 1, [((4, npt), F32), state, ((groups, *field), F32)],
        e, near_to(msg), far_to(msg), dissip, freqs, c, r, idx, gw, f0,
    )
    back = (-(-(dirs + 1) // n), *field)
    fields, own, *backs = phase(
        2, 2, [((16, npt), F32), ((dirs, *field), F32)] + [(back, F32)] * (n - 1),
        e, near_to(msg), far_to(msg), dissip, freqs, c, r, idx, gw, f0, f1,
    )
    energy, ordered = call(
        functools.partial(join_kernel, n, nfreq),
        [((dirs, nfreq, npt), F32), ((16, npt), F32)],
        [],
        own, fields, send_order, *[swap(x, d) for d, x in zip(peers, backs)],
    )
    if tiles <= 4:
        others = [lax.ppermute(ordered, "space", [(t, (t + d) % tiles) for t in range(tiles)]) for d in range(1, tiles)]
        (series,) = call(functools.partial(hand_kernel, tiles), [((2 * STEPS, npt), F32)], [], ordered, *others)
    else:
        parts = ordered[: 2 * STEPS].reshape(2 * STEPS, tiles, npt // tiles)
        series = lax.all_to_all(parts, "space", split_axis=1, concat_axis=1, tiled=True).reshape(2 * STEPS, npt)
    return (energy, series)


def solution(mesh):
    placed = (
        P("spec", None, ("runs", "space")),
        P("spec", None, "space"),
        P("spec", None, "space"),
        P(None, ("runs", "space")),
        P(),
        P("spec", "space"),
        P("space"),
    )
    return jax.shard_map(
        on_device,
        mesh=mesh,
        in_specs=placed,
        out_specs=(P("spec", None, ("runs", "space")), P(None, ("runs", "space"))),
        check_vma=False,
    )
```

```python
import functools

import jax
import jax.numpy as jnp
from jax import lax
from jax.experimental import pallas as pl
from jax.experimental.pallas import tpu as pltpu
from jax.sharding import PartitionSpec as P

STEPS = 6
ROWS = 40
F32 = jnp.float32


def frequency_table(count):
    return 0.035 * jnp.float32(1.1) ** jnp.arange(count, dtype=jnp.float32)


def subtile_of(s, k, n):
    return jnp.where(s % 2 == 0, k, n - 1 - k)


def far_route(tiles, n):
    route = []
    for s in range(tiles):
        for k in range(n):
            q = k if s % 2 == 0 else n - 1 - k
            at = s * n + q
            to = (at - 1 if q % 2 == 0 else at + 1) % (tiles * n)
            ts, tq = divmod(to, n)
            route.append((s * n + k, ts * n + (tq if ts % 2 == 0 else n - 1 - tq)))
    return route


def lanes(shape):
    return lax.broadcasted_iota(jnp.int32, shape, len(shape) - 1)


class Spot:
    def __init__(self, n, npt):
        self.n, self.sub, self.npt = n, npt // n, npt
        self.s, self.k = lax.axis_index("space"), lax.axis_index("spec")
        self.q = subtile_of(self.s, self.k, n)
        self.qn = self.q ^ 1
        self.qf = n - 1 - self.q
        self.even = self.q % 2 == 0

    def shift(self, to, frm):
        return ((to - frm + self.n) % self.n) * self.sub

    def block(self, shape):
        return lanes(shape) // self.sub


def move(x, amount):
    return pltpu.roll(x, amount, 1)


def offsets(upwind, s, npt, total, reach):
    own = s * npt + lanes(upwind.shape)
    return (jnp.mod(upwind - own + reach, total) - reach).astype(F32)


def pieces(dirs, n):
    full = (dirs - 1) // n
    where = []
    for b in range(n):
        where += [(full * b + j // n, j % n) for j in range(dirs - 1)] + [(full * n, b)]
    return where


def pack_kernel(n, total, reach, e_hbm, c_hbm, r_hbm, u_hbm, *rest):
    outs, (e_ref, c_ref, r_ref, u_ref, v, sem) = rest[:n], rest[n:]
    dirs, nfreq, npt = e_ref.shape
    copies = [
        pltpu.make_async_copy(x, y, sem.at[i])
        for i, (x, y) in enumerate(((e_hbm, e_ref), (c_hbm, c_ref), (r_hbm, r_ref), (u_hbm, u_ref)))
    ]
    for copy in copies:
        copy.start()
    for copy in copies:
        copy.wait()
    at = Spot(n, npt)
    off = offsets(u_ref[...], at.s, npt, total, reach)
    for a, ref in enumerate((e_ref, c_ref, r_ref)):
        for j in range(dirs):
            v[a * dirs + j, :nfreq, :] = ref[j]
            v[a * dirs + j, nfreq:, :] = jnp.broadcast_to(off[j : j + 1], (ROWS - nfreq, npt))
    block = at.block((ROWS, npt))
    full = (dirs - 1) // n
    last = [(at.k + a) % n for a in range(3)]
    for d in range(n):
        to = subtile_of(at.s, at.k ^ d, n)
        for a in range(3):
            for h in range(full):
                row = None
                for i in range(n):
                    piece = move(v[a * dirs + n * h + i], at.shift(i, to))
                    row = piece if row is None else jnp.where(block == i, piece, row)
                outs[d][full * a + h] = row
        row = None
        for a in range(3):
            piece = move(v[(a + 1) * dirs - 1], at.shift(last[a], to))
            row = piece if row is None else jnp.where(block == last[a], piece, row)
        outs[d][3 * full] = row


def spread_kernel(n, g_ref, *rest):
    msgs, (pe, pc, pr, near, far) = rest[:n], rest[n:]
    rows, npt = msgs[0].shape[1:]
    nfreq = g_ref.shape[0]
    at = Spot(n, npt)
    full = (msgs[0].shape[0] - 1) // 3
    block = at.block((rows, npt))
    half = at.sub // 2
    low = lanes((rows, npt)) % at.sub < half
    for a, out in enumerate((pe, pc, pr)):
        row = None
        for d in range(n):
            b = at.k ^ d
            for h in range(full):
                out[full * b + h] = msgs[d][full * a + h]
            left = msgs[d][3 * full]
            row = left if row is None else jnp.where(block == (b + a) % n, left, row)
        out[full * n] = move(row, npt - a * at.sub) if a else row
    slabs = full * n + 1
    for out, first in ((near, jnp.logical_not(at.even)), (far, at.even)):
        keep = jnp.logical_xor(low, jnp.logical_not(first))
        amount = jnp.where(first, half, npt - half)
        for g in range(slabs):
            out[g] = pe[g]
            out[slabs + g] = jnp.where(keep, pc[g], move(pr[g], amount))
    far[2 * slabs, :nfreq, :] = g_ref[...]
    far[2 * slabs, nfreq:, :] = jnp.zeros((rows - nfreq, npt), F32)


def window(at, own, near, far, base, nback, fback, out, where, block):
    dn, df = at.shift(at.qn, at.q), at.shift(at.qf, at.q)
    dn, df = (dn + nback) % at.npt, (df + fback) % at.npt
    step = (at.qn - at.q + at.n) % at.n
    for g in range(own.shape[0]):
        x, y, z = own[g], move(near[base + g], dn), move(far[base + g], df)
        for d, (slab, i) in enumerate(where):
            if slab == g:
                both = jnp.where(block == i, x, jnp.where(block == (i + step) % at.n, y, z))
                out[d] = move(both, at.shift(at.q, i))


def hour(e, c, r, idx, out, m0s, grow1, dissip, freqs, bins, nfreq, factor):
    ndir, rows, npt = e.shape

    def moved(d):
        x = e[d]
        if factor is not None:
            x = x * factor
        index = jnp.broadcast_to(idx[pl.ds(d, 1), :], (rows, npt))
        up = jnp.take_along_axis(x, index, axis=1)
        return x + c[d] * (up - x)

    def flux(d, here, there):
        rate = r[d]
        return rate * jnp.where(rate > 0.0, here, there)

    first = moved(0)
    m0s[...] = first
    last = moved(ndir - 1)

    def body(d, carry):
        here, before, total = carry
        there = moved(d + 1)
        f = flux(d, here, there)
        turned = here - f + before
        out[d] = turned
        return there, f, total + turned

    here, before, total = lax.fori_loop(
        0, ndir - 1, body, (first, flux(ndir - 1, last, first), jnp.zeros((rows, npt), F32)), unroll=True
    )
    f = flux(ndir - 1, here, m0s[...])
    turned = here - f + before
    out[ndir - 1] = turned
    total = total + turned
    live = lax.broadcasted_iota(jnp.int32, (rows, npt), 0) < nfreq
    total = jnp.where(live, total, 0.0)
    mean = jnp.sum(total, axis=0, keepdims=True) / bins
    factor = grow1 / (1.0 + dissip * mean)
    part = jnp.where(live, factor * total, 0.0)
    zeroth = jnp.sum(part, axis=0, keepdims=True)
    first_moment = jnp.sum(part * freqs, axis=0, keepdims=True)
    return factor, 4.0 * jnp.sqrt(zeroth / bins), zeroth / first_moment


def phase_kernel(n, stage, bins, nfreq, fields_before, *refs):
    refs = list(refs)
    take = lambda count: [refs.pop(0) for _ in range(count)]
    own, near, far, dissip_ref, freqs_ref = take(5)
    if stage == 0:
        pc, pr, g_ref = take(3)
    else:
        cw, rw, idx, gw = take(4)
        old = take(fields_before)
    if stage == 0:
        cw, rw, idx, gw = take(4)
    fields = take(1)[0]
    if stage < 2:
        msg = take(1)[0]
    else:
        eo = take(1)[0]
        backs = take(n - 1)
    ew, et, m0s = take(3)
    ndir, rows, npt = ew.shape
    dirs = ndir // n
    at = Spot(n, npt)
    shape = (rows, npt)
    block = at.block(shape)
    where = pieces(dirs, n)
    slabs = own.shape[0]
    window(at, own, near, far, 0, 0, 0, ew, where, block)
    if stage == 0:
        half = at.sub // 2
        nback, fback = jnp.where(at.even, npt - half, half), jnp.where(at.even, half, npt - half)
        window(at, pc, near, far, slabs, 0, 0, cw, where, block)
        window(at, pr, near, far, slabs, nback, fback, rw, where, block)
        m0s[...] = jnp.zeros(shape, F32)
        for d in range(ndir):
            m0s[d : d + 1, :] = ew[d, nfreq : nfreq + 1, :]
        idx[...] = (lanes(shape) + m0s[...].astype(jnp.int32)) & (npt - 1)
        gw[:nfreq, :] = 1.0 + jnp.where(block[:nfreq] == at.qf, far[2 * slabs, :nfreq, :], g_ref[...])
        gw[nfreq:, :] = jnp.ones((rows - nfreq, npt), F32)
    grow1, dissip, freqs = gw[...], dissip_ref[...], freqs_ref[...]
    fa, ha, pa = hour(ew, cw, rw, idx, et, m0s, grow1, dissip, freqs, bins, nfreq, None)
    fb, hb, pb = hour(et, cw, rw, idx, ew, m0s, grow1, dissip, freqs, bins, nfreq, fa)
    if stage < 2:
        fields[...] = jnp.concatenate([ha, hb, pa, pb], axis=0)
        for g in range(slabs):
            row = None
            for d, (slab, i) in enumerate(where):
                if slab == g:
                    piece = move(ew[d] * fb, at.shift(i, at.q))
                    row = piece if row is None else jnp.where(block == i, piece, row)
            msg[g] = row
    else:
        h = [o[:2] for o in old] + [ha, hb]
        p = [o[2:] for o in old] + [pa, pb]
        every = jnp.concatenate(h + p + [jnp.zeros((16 - 2 * STEPS, npt), F32)], axis=0)
        fields[...] = every
        for j in range(dirs):
            eo[j] = ew[dirs * at.k + j] * fb
        m0s[...] = jnp.zeros(shape, F32)
        m0s[:16, :] = every
        tail = m0s[...]
        for d in range(1, n):
            b = at.k ^ d
            for g in range(backs[0].shape[0]):
                row = None
                for i in range(n):
                    j = n * g + i
                    if j > dirs:
                        continue
                    x = ew[dirs * b + j] * fb if j < dirs else tail
                    piece = move(x, at.shift(i, at.q))
                    row = piece if row is None else jnp.where(block == i, piece, row)
                backs[d - 1][g] = row


def order_kernel(n, dirs, f_ref, order_ref, *rest):
    msgs, series = rest[: n - 1], rest[n - 1]
    rows, npt = f_ref.shape
    at = Spot(n, npt)
    block = at.block((rows, npt))
    fields = f_ref[...]
    for d in range(1, n):
        q = subtile_of(at.s, at.k ^ d, n)
        piece = move(msgs[d - 1][dirs // n, :rows, :], at.shift(q, dirs % n))
        fields = jnp.where(block == q, piece, fields)
    index = jnp.broadcast_to((order_ref[...] - at.s * npt).reshape(1, npt), (rows, npt))
    series[...] = jnp.take_along_axis(fields, index, axis=1)


def join_kernel(n, e_ref, *rest):
    msgs, out = rest[: n - 1], rest[n - 1]
    dirs, rows, npt = e_ref.shape
    nfreq = out.shape[1]
    at = Spot(n, npt)
    block = at.block((rows, npt))
    qs = [subtile_of(at.s, at.k ^ d, n) for d in range(1, n)]
    for j in range(dirs):
        x = e_ref[j]
        for d in range(1, n):
            piece = move(msgs[d - 1][j // n], at.shift(qs[d - 1], j % n))
            x = jnp.where(block == qs[d - 1], piece, x)
        out[j] = x[:nfreq]


def hand_kernel(tiles, own_ref, *rest):
    others, out = rest[:-1], rest[-1]
    rows, npt = out.shape
    share = npt // tiles
    s = lax.axis_index("space")
    block = lanes((16, npt)) // share
    x = own_ref[...]
    for d in range(1, tiles):
        frm = s ^ d
        piece = move(others[d - 1][...], ((frm - s + tiles) % tiles) * share)
        x = jnp.where(block == frm, piece, x)
    out[...] = x[:rows]


def call(kernel, outs, scratch, *args, hbm=0):
    vm = pl.BlockSpec(memory_space=pltpu.VMEM)
    return pl.pallas_call(
        kernel,
        out_shape=[jax.ShapeDtypeStruct(shape, dtype) for shape, dtype in outs],
        in_specs=[pl.BlockSpec(memory_space=pltpu.HBM)] * hbm + [vm] * (len(args) - hbm),
        out_specs=[vm] * len(outs),
        scratch_shapes=scratch,
        compiler_params=pltpu.CompilerParams(vmem_limit_bytes=(54600 if hbm else 40960) * 1024),
    )(*args)


def on_device(spectrum, courant, refraction, growth, dissip, upwind, send_order):
    dirs, nfreq, npt = spectrum.shape
    tiles, n = lax.axis_size("space"), lax.axis_size("spec")
    total, reach = npt * tiles, npt // 8
    ndir = dirs * n
    bins = ndir * nfreq
    full = (dirs - 1) // n
    slabs = full * n + 1
    peers = range(1, n)
    swap = lambda x, d: lax.ppermute(x, "spec", [(k, k ^ d) for k in range(n)])
    near_to = lambda x: swap(x, 1)
    route = far_route(tiles, n)
    far_to = lambda x: lax.ppermute(x, ("space", "spec"), route)
    wide = lambda v: jnp.pad(jnp.broadcast_to(v[:, None], (nfreq, npt)), ((0, ROWS - nfreq), (0, 0)))
    freqs, dissip = wide(frequency_table(nfreq)), wide(dissip)
    field = (ROWS, npt)
    state, packed = ((ndir, *field), F32), ((slabs, *field), F32)

    part = pltpu.VMEM(spectrum.shape, F32)
    sent = call(
        functools.partial(pack_kernel, n, total, reach),
        [((3 * full + 1, *field), F32)] * n,
        [part, part, part, pltpu.VMEM(upwind.shape, jnp.int32), pltpu.VMEM((3 * dirs, *field), F32), pltpu.SemaphoreType.DMA((4,))],
        spectrum, courant, refraction, upwind, hbm=4,
    )
    got = [sent[0]] + [swap(sent[d], d) for d in peers]
    e, c, r, near, far = call(
        functools.partial(spread_kernel, n),
        [packed] * 3 + [((2 * slabs, *field), F32), ((2 * slabs + 1, *field), F32)],
        [],
        growth, *got,
    )
    scratch = [pltpu.VMEM(shape, F32) for shape in ((ndir, *field), (ndir, *field), field)]
    phase = lambda stage, before, outs, *args: call(
        functools.partial(phase_kernel, n, stage, bins, nfreq, before), outs, scratch, *args
    )
    some = ((4, npt), F32)
    c, r, idx, gw, f0, e = phase(
        0, 0, [state, state, (field, jnp.int32), (field, F32), some, packed],
        e, near_to(near), far_to(far), dissip, freqs, c, r, growth,
    )
    f1, e = phase(1, 1, [some, packed], e, near_to(e), far_to(e), dissip, freqs, c, r, idx, gw, f0)
    back = ((-(-(dirs + 1) // n), *field), F32)
    fields, own, *backs = phase(
        2, 2, [((16, npt), F32), ((dirs, *field), F32)] + [back] * (n - 1),
        e, near_to(e), far_to(e), dissip, freqs, c, r, idx, gw, f0, f1,
    )
    backs = [swap(x, d) for d, x in zip(peers, backs)]
    (ordered,) = call(functools.partial(order_kernel, n, dirs), [((16, npt), F32)], [], fields, send_order, *backs)
    (energy,) = call(functools.partial(join_kernel, n), [(spectrum.shape, F32)], [], own, *backs)
    if tiles == 4:
        others = [lax.ppermute(ordered, "space", [(t, t ^ d) for t in range(tiles)]) for d in range(1, tiles)]
        (series,) = call(functools.partial(hand_kernel, tiles), [((2 * STEPS, npt), F32)], [], ordered, *others)
    else:
        parts = ordered[: 2 * STEPS].reshape(2 * STEPS, tiles, npt // tiles)
        series = lax.all_to_all(parts, "space", split_axis=1, concat_axis=1, tiled=True).reshape(2 * STEPS, npt)
    return (energy, series)


def solution(mesh):
    placed = (
        P("spec", None, ("runs", "space")),
        P("spec", None, "space"),
        P("spec", None, "space"),
        P(None, ("runs", "space")),
        P(),
        P("spec", "space"),
        P("space"),
    )
    return jax.shard_map(
        on_device,
        mesh=mesh,
        in_specs=placed,
        out_specs=(P("spec", None, ("runs", "space")), P(None, ("runs", "space"))),
        check_vma=False,
    )
```

```python
import functools

import jax
import jax.numpy as jnp
from jax import lax
from jax.experimental import pallas as pl
from jax.experimental.pallas import tpu as pltpu
from jax.sharding import PartitionSpec as P

STEPS = 6
ROWS = 40
F32 = jnp.float32


def frequency_table(count):
    return 0.035 * jnp.float32(1.1) ** jnp.arange(count, dtype=jnp.float32)


def orders(tiles, n):
    up = list(range(n))
    if tiles == 4 and n == 4:
        return [up, [3, 1, 0, 2], [2, 0, 1, 3], up[::-1]]
    return [up if s % 2 == 0 else up[::-1] for s in range(tiles)]


def subtile_of(s, k, n):
    tiles = lax.axis_size("space")
    table = orders(tiles, n)
    if tiles != 4:
        return jnp.where(s % 2 == 0, k, n - 1 - k)
    q = k
    for t in range(1, tiles):
        here = n - 1
        for i in range(n - 1):
            here = jnp.where(k == table[t][i], i, here)
        q = jnp.where(s == t, here, q)
    return q


def ring_route(tiles, n, far):
    table = orders(tiles, n)
    route = []
    for s in range(tiles):
        for q in range(n):
            at = s * n + q
            to = (at + (1 if (q % 2 == 0) != far else -1)) % (tiles * n)
            route.append((s * n + table[s][q], to // n * n + table[to // n][to % n]))
    return route


def lanes(shape):
    return lax.broadcasted_iota(jnp.int32, shape, len(shape) - 1)


class Spot:
    def __init__(self, n, npt, q=None):
        self.n, self.sub, self.npt = n, npt // n, npt
        if q is None:
            self.s, self.k = lax.axis_index("space"), lax.axis_index("spec")
            q = subtile_of(self.s, self.k, n)
        self.q = q
        self.qn = self.q ^ 1
        self.qf = n - 1 - self.q
        self.even = self.q % 2 == 0

    def shift(self, to, frm):
        return ((to - frm + self.n) % self.n) * self.sub

    def block(self, shape):
        return lanes(shape) // self.sub

    def each(self, body):
        for q in range(self.n):
            pl.when(self.q == q)(functools.partial(body, Spot(self.n, self.npt, q)))


def move(x, amount):
    if isinstance(amount, int) and amount == 0:
        return x
    return pltpu.roll(x, amount, 1)


def offsets(upwind, s, npt, total, reach):
    own = s * npt + lanes(upwind.shape)
    return (jnp.mod(upwind - own + reach, total) - reach).astype(F32)


def pieces(dirs, n):
    full = (dirs - 1) // n
    where = []
    for b in range(n):
        where += [(full * b + j // n, j % n) for j in range(dirs - 1)] + [(full * n, b)]
    return where


def pack_kernel(n, total, reach, e_hbm, c_hbm, r_hbm, u_hbm, *rest):
    outs, (e_ref, c_ref, r_ref, u_ref, v, sem) = rest[:n], rest[n:]
    dirs, nfreq, npt = e_ref.shape
    copies = [
        pltpu.make_async_copy(x, y, sem.at[i])
        for i, (x, y) in enumerate(((e_hbm, e_ref), (c_hbm, c_ref), (r_hbm, r_ref), (u_hbm, u_ref)))
    ]
    for copy in copies:
        copy.start()
    for copy in copies:
        copy.wait()
    at = Spot(n, npt)
    off = offsets(u_ref[...], at.s, npt, total, reach)
    for a, ref in enumerate((e_ref, c_ref, r_ref)):
        for j in range(dirs):
            v[a * dirs + j, :nfreq, :] = ref[j]
            v[a * dirs + j, nfreq:, :] = jnp.broadcast_to(off[j : j + 1], (ROWS - nfreq, npt))
    block = at.block((ROWS, npt))
    full = (dirs - 1) // n
    last = [(at.k + a) % n for a in range(3)]
    for d in range(n):
        to = subtile_of(at.s, at.k ^ d, n)
        for a in range(3):
            for h in range(full):
                row = None
                for i in range(n):
                    piece = move(v[a * dirs + n * h + i], at.shift(i, to))
                    row = piece if row is None else jnp.where(block == i, piece, row)
                outs[d][full * a + h] = row
        row = None
        for a in range(3):
            piece = move(v[(a + 1) * dirs - 1], at.shift(last[a], to))
            row = piece if row is None else jnp.where(block == last[a], piece, row)
        outs[d][3 * full] = row


def spread_kernel(n, g_ref, *rest):
    msgs, (pe, pc, pr, near, far) = rest[:n], rest[n:]
    rows, npt = msgs[0].shape[1:]
    nfreq = g_ref.shape[0]
    at = Spot(n, npt)
    full = (msgs[0].shape[0] - 1) // 3
    block = at.block((rows, npt))
    half = at.sub // 2
    low = lanes((rows, npt)) % at.sub < half
    for a, out in enumerate((pe, pc, pr)):
        row = None
        for d in range(n):
            b = at.k ^ d
            for h in range(full):
                out[full * b + h] = msgs[d][full * a + h]
            left = msgs[d][3 * full]
            row = left if row is None else jnp.where(block == (b + a) % n, left, row)
        out[full * n] = move(row, npt - a * at.sub) if a else row
    slabs = full * n + 1
    def fill(even):
        for out, first in ((near, not even), (far, even)):
            for g in range(slabs):
                out[g] = pe[g]
                out[slabs + g] = jnp.where(low == first, pc[g], move(pr[g], half if first else npt - half))

    pl.when(at.even)(functools.partial(fill, True))
    pl.when(jnp.logical_not(at.even))(functools.partial(fill, False))
    far[2 * slabs, :nfreq, :] = g_ref[...]
    far[2 * slabs, nfreq:, :] = jnp.zeros((rows - nfreq, npt), F32)


def window(at, own, near, far, base, nback, fback, out, where, block, turned):
    dn, df = at.shift(at.qn, at.q), at.shift(at.qf, at.q)
    dn, df = (dn + nback) % at.npt, (df + fback) % at.npt
    step = (at.qn - at.q + at.n) % at.n
    slabs = own.shape[0]
    for source, start, amount in ((near, 0, dn), (far, slabs, df)):
        for g in range(slabs):
            turned[start + g] = move(source[base + g], amount)
    for i in range(at.n):
        here, side = block == i, block == (i + step) % at.n
        for d, (g, j) in enumerate(where):
            if i == j:
                out[d] = move(jnp.where(here, own[g], jnp.where(side, turned[g], turned[slabs + g])), at.shift(at.q, i))


def hour(e, c, r, idx, out, m0s, grow1, dissip, freqs, bins, nfreq, factor):
    ndir, rows, npt = e.shape

    def moved(d):
        x = e[d]
        if factor is not None:
            x = x * factor
        index = jnp.broadcast_to(idx[pl.ds(d, 1), :], (rows, npt))
        up = jnp.take_along_axis(x, index, axis=1)
        return x + c[d] * (up - x)

    def flux(d, here, there):
        rate = r[d]
        return rate * jnp.where(rate > 0.0, here, there)

    first = moved(0)
    m0s[...] = first
    last = moved(ndir - 1)

    def body(d, carry):
        here, before, total = carry
        there = moved(d + 1)
        f = flux(d, here, there)
        turned = here - f + before
        out[d] = turned
        return there, f, total + turned

    here, before, total = lax.fori_loop(
        0, ndir - 1, body, (first, flux(ndir - 1, last, first), jnp.zeros((rows, npt), F32)), unroll=True
    )
    f = flux(ndir - 1, here, m0s[...])
    turned = here - f + before
    out[ndir - 1] = turned
    total = total + turned
    live = lax.broadcasted_iota(jnp.int32, (rows, npt), 0) < nfreq
    total = jnp.where(live, total, 0.0)
    mean = jnp.sum(total, axis=0, keepdims=True) / bins
    factor = grow1 / (1.0 + dissip * mean)
    part = jnp.where(live, factor * total, 0.0)
    zeroth = jnp.sum(part, axis=0, keepdims=True)
    first_moment = jnp.sum(part * freqs, axis=0, keepdims=True)
    return factor, 4.0 * jnp.sqrt(zeroth / bins), zeroth / first_moment


def phase_kernel(n, stage, bins, nfreq, fields_before, *refs):
    refs = list(refs)
    take = lambda count: [refs.pop(0) for _ in range(count)]
    own, near, far, dissip_ref, freqs_ref = take(5)
    if stage == 0:
        pc, pr, g_ref = take(3)
    else:
        cw, rw, idx, gw = take(4)
        old = take(fields_before)
    if stage == 0:
        cw, rw, idx, gw = take(4)
    fields = take(1)[0]
    if stage < 2:
        msg = take(1)[0]
    else:
        eo = take(1)[0]
        backs = take(n - 1)
    ew, et, m0s = take(3)
    ndir, rows, npt = ew.shape
    dirs = ndir // n
    at = Spot(n, npt)
    shape = (rows, npt)
    block = at.block(shape)
    where = pieces(dirs, n)
    slabs = own.shape[0]

    def unpack(at):
        window(at, own, near, far, 0, 0, 0, ew, where, block, et)
        if stage == 0:
            half = at.sub // 2
            nback, fback = (npt - half, half) if at.even else (half, npt - half)
            window(at, pc, near, far, slabs, 0, 0, cw, where, block, et)
            window(at, pr, near, far, slabs, nback, fback, rw, where, block, et)

    at.each(unpack)
    if stage == 0:
        m0s[...] = jnp.zeros(shape, F32)
        for d in range(ndir):
            m0s[d : d + 1, :] = ew[d, nfreq : nfreq + 1, :]
        idx[...] = (lanes(shape) + m0s[...].astype(jnp.int32)) & (npt - 1)
        gw[:nfreq, :] = 1.0 + jnp.where(block[:nfreq] == at.qf, far[2 * slabs, :nfreq, :], g_ref[...])
        gw[nfreq:, :] = jnp.ones((rows - nfreq, npt), F32)
    grow1, dissip, freqs = gw[...], dissip_ref[...], freqs_ref[...]
    fa, ha, pa = hour(ew, cw, rw, idx, et, m0s, grow1, dissip, freqs, bins, nfreq, None)
    fb, hb, pb = hour(et, cw, rw, idx, ew, m0s, grow1, dissip, freqs, bins, nfreq, fa)
    if stage < 2:
        fields[...] = jnp.concatenate([ha, hb, pa, pb], axis=0)

        def pack(at):
            for g in range(slabs):
                row = None
                for d, (slab, i) in enumerate(where):
                    if slab == g:
                        piece = move(ew[d] * fb, at.shift(i, at.q))
                        row = piece if row is None else jnp.where(block == i, piece, row)
                msg[g] = row

        at.each(pack)
    else:
        h = [o[:2] for o in old] + [ha, hb]
        p = [o[2:] for o in old] + [pa, pb]
        every = jnp.concatenate(h + p + [jnp.zeros((16 - 2 * STEPS, npt), F32)], axis=0)
        fields[...] = every
        for j in range(dirs):
            eo[j] = ew[dirs * at.k + j] * fb
        m0s[...] = jnp.zeros(shape, F32)
        m0s[:16, :] = every
        tail = m0s[...]
        k = at.k

        def pack(at):
            for d in range(1, n):
                b = k ^ d
                for g in range(backs[0].shape[0]):
                    row = None
                    for i in range(n):
                        j = n * g + i
                        if j > dirs:
                            continue
                        x = ew[dirs * b + j] * fb if j < dirs else tail
                        piece = move(x, at.shift(i, at.q))
                        row = piece if row is None else jnp.where(block == i, piece, row)
                    backs[d - 1][g] = row

        at.each(pack)


def order_kernel(n, dirs, f_ref, order_ref, *rest):
    msgs, series = rest[: n - 1], rest[n - 1]
    rows, npt = f_ref.shape
    at = Spot(n, npt)
    block = at.block((rows, npt))
    fields = f_ref[...]
    for d in range(1, n):
        q = subtile_of(at.s, at.k ^ d, n)
        piece = move(msgs[d - 1][dirs // n, :rows, :], at.shift(q, dirs % n))
        fields = jnp.where(block == q, piece, fields)
    index = jnp.broadcast_to((order_ref[...] - at.s * npt).reshape(1, npt), (rows, npt))
    series[...] = jnp.take_along_axis(fields, index, axis=1)


def join_kernel(n, e_ref, *rest):
    msgs, out = rest[: n - 1], rest[n - 1]
    dirs, rows, npt = e_ref.shape
    nfreq = out.shape[1]
    at = Spot(n, npt)
    block = at.block((rows, npt))
    qs = [subtile_of(at.s, at.k ^ d, n) for d in range(1, n)]
    for j in range(dirs):
        x = e_ref[j]
        for d in range(1, n):
            piece = move(msgs[d - 1][j // n], at.shift(qs[d - 1], j % n))
            x = jnp.where(block == qs[d - 1], piece, x)
        out[j] = x[:nfreq]


def hand_kernel(tiles, own_ref, *rest):
    others, out = rest[:-1], rest[-1]
    rows, npt = out.shape
    share = npt // tiles
    s = lax.axis_index("space")
    block = lanes((16, npt)) // share
    x = own_ref[...]
    for d in range(1, tiles):
        frm = s ^ d
        piece = move(others[d - 1][...], ((frm - s + tiles) % tiles) * share)
        x = jnp.where(block == frm, piece, x)
    out[...] = x[:rows]


def call(kernel, outs, scratch, *args, hbm=0):
    vm = pl.BlockSpec(memory_space=pltpu.VMEM)
    return pl.pallas_call(
        kernel,
        out_shape=[jax.ShapeDtypeStruct(shape, dtype) for shape, dtype in outs],
        in_specs=[pl.BlockSpec(memory_space=pltpu.HBM)] * hbm + [vm] * (len(args) - hbm),
        out_specs=[vm] * len(outs),
        scratch_shapes=scratch,
        compiler_params=pltpu.CompilerParams(vmem_limit_bytes=(54600 if hbm else 40960) * 1024),
    )(*args)


def on_device(spectrum, courant, refraction, growth, dissip, upwind, send_order):
    dirs, nfreq, npt = spectrum.shape
    tiles, n = lax.axis_size("space"), lax.axis_size("spec")
    total, reach = npt * tiles, npt // 8
    ndir = dirs * n
    bins = ndir * nfreq
    full = (dirs - 1) // n
    slabs = full * n + 1
    peers = range(1, n)
    swap = lambda x, d: lax.ppermute(x, "spec", [(k, k ^ d) for k in range(n)])
    near_to = lambda x: lax.ppermute(x, ("space", "spec"), ring_route(tiles, n, False))
    far_to = lambda x: lax.ppermute(x, ("space", "spec"), ring_route(tiles, n, True))
    wide = lambda v: jnp.pad(jnp.broadcast_to(v[:, None], (nfreq, npt)), ((0, ROWS - nfreq), (0, 0)))
    freqs, dissip = wide(frequency_table(nfreq)), wide(dissip)
    field = (ROWS, npt)
    state, packed = ((ndir, *field), F32), ((slabs, *field), F32)

    part = pltpu.VMEM(spectrum.shape, F32)
    sent = call(
        functools.partial(pack_kernel, n, total, reach),
        [((3 * full + 1, *field), F32)] * n,
        [part, part, part, pltpu.VMEM(upwind.shape, jnp.int32), pltpu.VMEM((3 * dirs, *field), F32), pltpu.SemaphoreType.DMA((4,))],
        spectrum, courant, refraction, upwind, hbm=4,
    )
    got = [sent[0]] + [swap(sent[d], d) for d in peers]
    e, c, r, near, far = call(
        functools.partial(spread_kernel, n),
        [packed] * 3 + [((2 * slabs, *field), F32), ((2 * slabs + 1, *field), F32)],
        [],
        growth, *got,
    )
    scratch = [pltpu.VMEM(shape, F32) for shape in ((ndir, *field), (ndir, *field), field)]
    phase = lambda stage, before, outs, *args: call(
        functools.partial(phase_kernel, n, stage, bins, nfreq, before), outs, scratch, *args
    )
    some = ((4, npt), F32)
    c, r, idx, gw, f0, e = phase(
        0, 0, [state, state, (field, jnp.int32), (field, F32), some, packed],
        e, near_to(near), far_to(far), dissip, freqs, c, r, growth,
    )
    f1, e = phase(1, 1, [some, packed], e, near_to(e), far_to(e), dissip, freqs, c, r, idx, gw, f0)
    back = ((-(-(dirs + 1) // n), *field), F32)
    fields, own, *backs = phase(
        2, 2, [((16, npt), F32), ((dirs, *field), F32)] + [back] * (n - 1),
        e, near_to(e), far_to(e), dissip, freqs, c, r, idx, gw, f0, f1,
    )
    backs = [swap(x, d) for d, x in zip(peers, backs)]
    (ordered,) = call(functools.partial(order_kernel, n, dirs), [((16, npt), F32)], [], fields, send_order, *backs)
    (energy,) = call(functools.partial(join_kernel, n), [(spectrum.shape, F32)], [], own, *backs)
    if tiles == 4:
        others = [lax.ppermute(ordered, "space", [(t, t ^ d) for t in range(tiles)]) for d in range(1, tiles)]
        (series,) = call(functools.partial(hand_kernel, tiles), [((2 * STEPS, npt), F32)], [], ordered, *others)
    else:
        parts = ordered[: 2 * STEPS].reshape(2 * STEPS, tiles, npt // tiles)
        series = lax.all_to_all(parts, "space", split_axis=1, concat_axis=1, tiled=True).reshape(2 * STEPS, npt)
    return (energy, series)


def solution(mesh):
    placed = (
        P("spec", None, ("runs", "space")),
        P("spec", None, "space"),
        P("spec", None, "space"),
        P(None, ("runs", "space")),
        P(),
        P("spec", "space"),
        P("space"),
    )
    return jax.shard_map(
        on_device,
        mesh=mesh,
        in_specs=placed,
        out_specs=(P("spec", None, ("runs", "space")), P(None, ("runs", "space"))),
        check_vma=False,
    )
```

```python
import functools

import jax
import jax.numpy as jnp
from jax import lax
from jax.experimental import pallas as pl
from jax.experimental.pallas import tpu as pltpu
from jax.sharding import PartitionSpec as P

STEPS = 6
ROWS = 40
F32 = jnp.float32


def frequency_table(count):
    return 0.035 * jnp.float32(1.1) ** jnp.arange(count, dtype=jnp.float32)


def orders(tiles, n):
    up = list(range(n))
    if tiles == 4 and n == 4:
        return [up, [3, 1, 0, 2], [2, 0, 1, 3], up[::-1]]
    return [up if s % 2 == 0 else up[::-1] for s in range(tiles)]


def subtile_of(s, k, n):
    tiles = lax.axis_size("space")
    table = orders(tiles, n)
    if tiles != 4:
        return jnp.where(s % 2 == 0, k, n - 1 - k)
    q = k
    for t in range(1, tiles):
        here = n - 1
        for i in range(n - 1):
            here = jnp.where(k == table[t][i], i, here)
        q = jnp.where(s == t, here, q)
    return q


def ring_route(tiles, n, far):
    table = orders(tiles, n)
    route = []
    for s in range(tiles):
        for q in range(n):
            at = s * n + q
            to = (at + (1 if (q % 2 == 0) != far else -1)) % (tiles * n)
            route.append((s * n + table[s][q], to // n * n + table[to // n][to % n]))
    return route


def lanes(shape):
    return lax.broadcasted_iota(jnp.int32, shape, len(shape) - 1)


class Spot:
    def __init__(self, n, npt, q=None):
        self.n, self.sub, self.npt = n, npt // n, npt
        if q is None:
            self.s, self.k = lax.axis_index("space"), lax.axis_index("spec")
            q = subtile_of(self.s, self.k, n)
        self.q = q
        self.qn = self.q ^ 1
        self.qf = n - 1 - self.q
        self.even = self.q % 2 == 0

    def shift(self, to, frm):
        return ((to - frm + self.n) % self.n) * self.sub

    def block(self, shape):
        return lanes(shape) // self.sub

    def each(self, body):
        for q in range(self.n):
            pl.when(self.q == q)(functools.partial(body, Spot(self.n, self.npt, q)))


def move(x, amount):
    if isinstance(amount, int) and amount == 0:
        return x
    return pltpu.roll(x, amount, 1)


def offsets(upwind, s, npt, total, reach):
    own = s * npt + lanes(upwind.shape)
    return (jnp.mod(upwind - own + reach, total) - reach).astype(F32)


def pieces(dirs, n):
    full = (dirs - 1) // n
    where = []
    for b in range(n):
        where += [(full * b + j // n, j % n) for j in range(dirs - 1)] + [(full * n, b)]
    return where


def pack_kernel(n, e_hbm, c_hbm, r_hbm, *rest):
    outs, (e_ref, c_ref, r_ref, sem) = rest[:n], rest[n:]
    dirs, nfreq, npt = e_ref.shape
    copies = [
        pltpu.make_async_copy(x, y, sem.at[i])
        for i, (x, y) in enumerate(((e_hbm, e_ref), (c_hbm, c_ref), (r_hbm, r_ref)))
    ]
    for copy in copies:
        copy.start()
    for copy in copies:
        copy.wait()
    at = Spot(n, npt)
    block = at.block((nfreq, npt))
    full = (dirs - 1) // n
    last = [(at.k + a) % n for a in range(3)]
    for d in range(n):
        to = subtile_of(at.s, at.k ^ d, n)
        for a, ref in enumerate((e_ref, c_ref, r_ref)):
            for h in range(full):
                row = None
                for i in range(n):
                    piece = move(ref[n * h + i], at.shift(i, to))
                    row = piece if row is None else jnp.where(block == i, piece, row)
                outs[d][full * a + h, :nfreq, :] = row
        row = None
        for a, ref in enumerate((e_ref, c_ref, r_ref)):
            piece = move(ref[dirs - 1], at.shift(last[a], to))
            row = piece if row is None else jnp.where(block == last[a], piece, row)
        outs[d][3 * full, :nfreq, :] = row


def offset_kernel(n, nfreq, total, reach, u_ref, *refs):
    outs = refs[n:]
    dirs, npt = u_ref.shape
    at = Spot(n, npt)
    off = offsets(u_ref[...], at.s, npt, total, reach)
    block = at.block((1, npt))
    full = (dirs - 1) // n
    for d in range(n):
        to = subtile_of(at.s, at.k ^ d, n)
        turned = [move(off, at.shift(i, to)) for i in range(n)]
        for h in range(full):
            row = turned[0][n * h : n * h + 1]
            for i in range(1, n):
                row = jnp.where(block == i, turned[i][n * h + i : n * h + i + 1], row)
            outs[d][h, nfreq : nfreq + 1, :] = row
        row = move(off, at.shift(at.k, to))[dirs - 1 : dirs]
        outs[d][3 * full, nfreq : nfreq + 1, :] = row


def spread_kernel(n, g_ref, *rest):
    msgs, (pe, pc, pr, near, far) = rest[:n], rest[n:]
    rows, npt = msgs[0].shape[1:]
    nfreq = g_ref.shape[0]
    at = Spot(n, npt)
    full = (msgs[0].shape[0] - 1) // 3
    block = at.block((rows, npt))
    half = at.sub // 2
    low = lanes((rows, npt)) % at.sub < half
    for a, out in enumerate((pe, pc, pr)):
        row = None
        for d in range(n):
            b = at.k ^ d
            for h in range(full):
                out[full * b + h] = msgs[d][full * a + h]
            left = msgs[d][3 * full]
            row = left if row is None else jnp.where(block == (b + a) % n, left, row)
        out[full * n] = move(row, npt - a * at.sub) if a else row
    slabs = full * n + 1
    def fill(even):
        for out, first in ((near, not even), (far, even)):
            for g in range(slabs):
                out[g] = pe[g]
                out[slabs + g] = jnp.where(low == first, pc[g], move(pr[g], half if first else npt - half))

    pl.when(at.even)(functools.partial(fill, True))
    pl.when(jnp.logical_not(at.even))(functools.partial(fill, False))
    far[2 * slabs, :nfreq, :] = g_ref[...]
    far[2 * slabs, nfreq:, :] = jnp.zeros((rows - nfreq, npt), F32)


def window(at, own, near, far, base, nback, fback, out, where, block, turned):
    dn, df = at.shift(at.qn, at.q), at.shift(at.qf, at.q)
    dn, df = (dn + nback) % at.npt, (df + fback) % at.npt
    step = (at.qn - at.q + at.n) % at.n
    slabs = own.shape[0]
    for source, start, amount in ((near, 0, dn), (far, slabs, df)):
        for g in range(slabs):
            turned[start + g] = move(source[base + g], amount)
    for i in range(at.n):
        here, side = block == i, block == (i + step) % at.n
        for d, (g, j) in enumerate(where):
            if i == j:
                out[d] = move(jnp.where(here, own[g], jnp.where(side, turned[g], turned[slabs + g])), at.shift(at.q, i))


def hour(e, c, r, idx, out, m0s, grow1, dissip, freqs, bins, nfreq, factor):
    ndir, rows, npt = e.shape

    def moved(d):
        x = e[d]
        if factor is not None:
            x = x * factor
        index = jnp.broadcast_to(idx[pl.ds(d, 1), :], (rows, npt))
        up = jnp.take_along_axis(x, index, axis=1)
        return x + c[d] * (up - x)

    def flux(d, here, there):
        rate = r[d]
        return rate * jnp.where(rate > 0.0, here, there)

    first = moved(0)
    m0s[...] = first
    last = moved(ndir - 1)

    def body(d, carry):
        here, before, total = carry
        there = moved(d + 1)
        f = flux(d, here, there)
        turned = here - f + before
        out[d] = turned
        return there, f, total + turned

    here, before, total = lax.fori_loop(
        0, ndir - 1, body, (first, flux(ndir - 1, last, first), jnp.zeros((rows, npt), F32)), unroll=True
    )
    f = flux(ndir - 1, here, m0s[...])
    turned = here - f + before
    out[ndir - 1] = turned
    total = total + turned
    live = lax.broadcasted_iota(jnp.int32, (rows, npt), 0) < nfreq
    total = jnp.where(live, total, 0.0)
    mean = jnp.sum(total, axis=0, keepdims=True) / bins
    factor = grow1 / (1.0 + dissip * mean)
    part = jnp.where(live, factor * total, 0.0)
    zeroth = jnp.sum(part, axis=0, keepdims=True)
    first_moment = jnp.sum(part * freqs, axis=0, keepdims=True)
    return factor, 4.0 * jnp.sqrt(zeroth / bins), zeroth / first_moment


def phase_kernel(n, stage, bins, nfreq, fields_before, *refs):
    refs = list(refs)
    take = lambda count: [refs.pop(0) for _ in range(count)]
    own, near, far, table_ref = take(4)
    if stage == 0:
        pc, pr, g_ref = take(3)
    else:
        cw, rw, idx, gw = take(4)
        old = take(fields_before)
    if stage == 0:
        cw, rw, idx, gw = take(4)
    fields = take(1)[0]
    if stage < 2:
        msg = take(1)[0]
    else:
        eo = take(1)[0]
        backs = take(n - 1)
    ew, et, m0s = take(3)
    ndir, rows, npt = ew.shape
    dirs = ndir // n
    at = Spot(n, npt)
    shape = (rows, npt)
    block = at.block(shape)
    where = pieces(dirs, n)
    slabs = own.shape[0]

    def unpack(at):
        window(at, own, near, far, 0, 0, 0, ew, where, block, et)
        if stage == 0:
            half = at.sub // 2
            nback, fback = (npt - half, half) if at.even else (half, npt - half)
            window(at, pc, near, far, slabs, 0, 0, cw, where, block, et)
            window(at, pr, near, far, slabs, nback, fback, rw, where, block, et)

    at.each(unpack)
    if stage == 0:
        m0s[...] = jnp.zeros(shape, F32)
        for d in range(ndir):
            m0s[d : d + 1, :] = ew[d, nfreq : nfreq + 1, :]
        idx[...] = (lanes(shape) + m0s[...].astype(jnp.int32)) & (npt - 1)
        gw[:nfreq, :] = 1.0 + jnp.where(block[:nfreq] == at.qf, far[2 * slabs, :nfreq, :], g_ref[...])
        gw[nfreq:, :] = jnp.ones((rows - nfreq, npt), F32)
    grow1, dissip, freqs = gw[...], table_ref[0], table_ref[1]
    fa, ha, pa = hour(ew, cw, rw, idx, et, m0s, grow1, dissip, freqs, bins, nfreq, None)
    fb, hb, pb = hour(et, cw, rw, idx, ew, m0s, grow1, dissip, freqs, bins, nfreq, fa)
    if stage < 2:
        fields[...] = jnp.concatenate([ha, hb, pa, pb], axis=0)

        def pack(at):
            for g in range(slabs):
                row = None
                for d, (slab, i) in enumerate(where):
                    if slab == g:
                        piece = move(ew[d] * fb, at.shift(i, at.q))
                        row = piece if row is None else jnp.where(block == i, piece, row)
                msg[g] = row

        at.each(pack)
    else:
        h = [o[:2] for o in old] + [ha, hb]
        p = [o[2:] for o in old] + [pa, pb]
        every = jnp.concatenate(h + p + [jnp.zeros((16 - 2 * STEPS, npt), F32)], axis=0)
        fields[...] = every
        for j in range(dirs):
            eo[j] = ew[dirs * at.k + j] * fb
        m0s[...] = jnp.zeros(shape, F32)
        m0s[:16, :] = every
        tail = m0s[...]
        k = at.k

        def pack(at):
            for d in range(1, n):
                b = k ^ d
                for g in range(backs[0].shape[0]):
                    row = None
                    for i in range(n):
                        j = n * g + i
                        if j > dirs:
                            continue
                        x = ew[dirs * b + j] * fb if j < dirs else tail
                        piece = move(x, at.shift(i, at.q))
                        row = piece if row is None else jnp.where(block == i, piece, row)
                    backs[d - 1][g] = row

        at.each(pack)


def order_kernel(n, dirs, f_ref, order_ref, *rest):
    msgs, series = rest[: n - 1], rest[n - 1]
    rows, npt = f_ref.shape
    at = Spot(n, npt)
    block = at.block((rows, npt))
    fields = f_ref[...]
    for d in range(1, n):
        q = subtile_of(at.s, at.k ^ d, n)
        piece = move(msgs[d - 1][dirs // n, :rows, :], at.shift(q, dirs % n))
        fields = jnp.where(block == q, piece, fields)
    index = jnp.broadcast_to((order_ref[...] - at.s * npt).reshape(1, npt), (rows, npt))
    series[...] = jnp.take_along_axis(fields, index, axis=1)


def join_kernel(n, e_ref, *rest):
    msgs, out = rest[: n - 1], rest[n - 1]
    dirs, rows, npt = e_ref.shape
    nfreq = out.shape[1]
    at = Spot(n, npt)
    block = at.block((rows, npt))
    qs = [subtile_of(at.s, at.k ^ d, n) for d in range(1, n)]
    for j in range(dirs):
        x = e_ref[j]
        for d in range(1, n):
            piece = move(msgs[d - 1][j // n], at.shift(qs[d - 1], j % n))
            x = jnp.where(block == qs[d - 1], piece, x)
        out[j] = x[:nfreq]


def hand_kernel(tiles, own_ref, *rest):
    others, out = rest[:-1], rest[-1]
    rows, npt = out.shape
    share = npt // tiles
    s = lax.axis_index("space")
    block = lanes((16, npt)) // share
    x = own_ref[...]
    for d in range(1, tiles):
        frm = s ^ d
        piece = move(others[d - 1][...], ((frm - s + tiles) % tiles) * share)
        x = jnp.where(block == frm, piece, x)
    out[...] = x[:rows]


def call(kernel, outs, scratch, *args, hbm=0, alias=None):
    vm = pl.BlockSpec(memory_space=pltpu.VMEM)
    return pl.pallas_call(
        kernel,
        out_shape=[jax.ShapeDtypeStruct(shape, dtype) for shape, dtype in outs],
        in_specs=[pl.BlockSpec(memory_space=pltpu.HBM)] * hbm + [vm] * (len(args) - hbm),
        out_specs=[vm] * len(outs),
        scratch_shapes=scratch,
        input_output_aliases=alias or {},
        compiler_params=pltpu.CompilerParams(vmem_limit_bytes=(54600 if hbm else 40960) * 1024),
    )(*args)


def on_device(spectrum, courant, refraction, growth, dissip, upwind, send_order):
    dirs, nfreq, npt = spectrum.shape
    tiles, n = lax.axis_size("space"), lax.axis_size("spec")
    total, reach = npt * tiles, npt // 8
    ndir = dirs * n
    bins = ndir * nfreq
    full = (dirs - 1) // n
    slabs = full * n + 1
    peers = range(1, n)
    swap = lambda x, d: lax.ppermute(x, "spec", [(k, k ^ d) for k in range(n)])
    near_to = lambda x: lax.ppermute(x, ("space", "spec"), ring_route(tiles, n, False))
    far_to = lambda x: lax.ppermute(x, ("space", "spec"), ring_route(tiles, n, True))
    table = jnp.stack([dissip, frequency_table(nfreq)])
    table = jnp.broadcast_to(jnp.pad(table, ((0, 0), (0, ROWS - nfreq)))[:, :, None], (2, ROWS, npt))
    field = (ROWS, npt)
    state, packed = ((ndir, *field), F32), ((slabs, *field), F32)

    part = pltpu.VMEM(spectrum.shape, F32)
    sent = call(
        functools.partial(pack_kernel, n),
        [((3 * full + 1, *field), F32)] * n,
        [part, part, part, pltpu.SemaphoreType.DMA((3,))],
        spectrum, courant, refraction, hbm=3,
    )
    sent = call(
        functools.partial(offset_kernel, n, nfreq, total, reach),
        [((3 * full + 1, *field), F32)] * n,
        [],
        upwind, *sent, alias={1 + d: d for d in range(n)},
    )
    got = [sent[0]] + [swap(sent[d], d) for d in peers]
    e, c, r, near, far = call(
        functools.partial(spread_kernel, n),
        [packed] * 3 + [((2 * slabs, *field), F32), ((2 * slabs + 1, *field), F32)],
        [],
        growth, *got,
    )
    scratch = [pltpu.VMEM(shape, F32) for shape in ((ndir, *field), (ndir, *field), field)]
    phase = lambda stage, before, outs, *args: call(
        functools.partial(phase_kernel, n, stage, bins, nfreq, before), outs, scratch, *args
    )
    some = ((4, npt), F32)
    c, r, idx, gw, f0, e = phase(
        0, 0, [state, state, (field, jnp.int32), (field, F32), some, packed],
        e, near_to(near), far_to(far), table, c, r, growth,
    )
    f1, e = phase(1, 1, [some, packed], e, near_to(e), far_to(e), table, c, r, idx, gw, f0)
    back = ((-(-(dirs + 1) // n), *field), F32)
    fields, own, *backs = phase(
        2, 2, [((16, npt), F32), ((dirs, *field), F32)] + [back] * (n - 1),
        e, near_to(e), far_to(e), table, c, r, idx, gw, f0, f1,
    )
    backs = [swap(x, d) for d, x in zip(peers, backs)]
    (ordered,) = call(functools.partial(order_kernel, n, dirs), [((16, npt), F32)], [], fields, send_order, *backs)
    (energy,) = call(functools.partial(join_kernel, n), [(spectrum.shape, F32)], [], own, *backs)
    if tiles == 4:
        others = [lax.ppermute(ordered, "space", [(t, t ^ d) for t in range(tiles)]) for d in range(1, tiles)]
        (series,) = call(functools.partial(hand_kernel, tiles), [((2 * STEPS, npt), F32)], [], ordered, *others)
    else:
        parts = ordered[: 2 * STEPS].reshape(2 * STEPS, tiles, npt // tiles)
        series = lax.all_to_all(parts, "space", split_axis=1, concat_axis=1, tiled=True).reshape(2 * STEPS, npt)
    return (energy, series)


def solution(mesh):
    placed = (
        P("spec", None, ("runs", "space")),
        P("spec", None, "space"),
        P("spec", None, "space"),
        P(None, ("runs", "space")),
        P(),
        P("spec", "space"),
        P("space"),
    )
    return jax.shard_map(
        on_device,
        mesh=mesh,
        in_specs=placed,
        out_specs=(P("spec", None, ("runs", "space")), P(None, ("runs", "space"))),
        check_vma=False,
    )
```

```python
import functools

import jax
import jax.numpy as jnp
from jax import lax
from jax.experimental import pallas as pl
from jax.experimental.pallas import tpu as pltpu
from jax.sharding import PartitionSpec as P

STEPS = 6
ROWS = 40
F32 = jnp.float32


def frequency_table(count):
    return 0.035 * jnp.float32(1.1) ** jnp.arange(count, dtype=jnp.float32)


def orders(tiles, n):
    up = list(range(n))
    if tiles == 4 and n == 4:
        return [up, [3, 0, 1, 2], [2, 1, 0, 3], up[::-1]]
    return [up if s % 2 == 0 else up[::-1] for s in range(tiles)]


def subtile_of(s, k, n):
    tiles = lax.axis_size("space")
    table = orders(tiles, n)
    if tiles != 4:
        return jnp.where(s % 2 == 0, k, n - 1 - k)
    q = k
    for t in range(1, tiles):
        here = n - 1
        for i in range(n - 1):
            here = jnp.where(k == table[t][i], i, here)
        q = jnp.where(s == t, here, q)
    return q


def ring_route(tiles, n, far):
    table = orders(tiles, n)
    route = []
    for s in range(tiles):
        for q in range(n):
            at = s * n + q
            to = (at + (1 if (q % 2 == 0) != far else -1)) % (tiles * n)
            route.append((s * n + table[s][q], to // n * n + table[to // n][to % n]))
    return route


def lanes(shape):
    return lax.broadcasted_iota(jnp.int32, shape, len(shape) - 1)


class Spot:
    def __init__(self, n, npt, q=None):
        self.n, self.sub, self.npt = n, npt // n, npt
        if q is None:
            self.s, self.k = lax.axis_index("space"), lax.axis_index("spec")
            q = subtile_of(self.s, self.k, n)
        self.q = q
        self.qn = self.q ^ 1
        self.qf = n - 1 - self.q
        self.even = self.q % 2 == 0

    def shift(self, to, frm):
        return ((to - frm + self.n) % self.n) * self.sub

    def block(self, shape):
        return lanes(shape) // self.sub

    def each(self, body):
        for q in range(self.n):
            pl.when(self.q == q)(functools.partial(body, Spot(self.n, self.npt, q)))


def move(x, amount):
    if isinstance(amount, int) and amount == 0:
        return x
    return pltpu.roll(x, amount, 1)


def offsets(upwind, s, npt, total, reach):
    own = s * npt + lanes(upwind.shape)
    return (jnp.mod(upwind - own + reach, total) - reach).astype(F32)


def pieces(dirs, n):
    full = (dirs - 1) // n
    where = []
    for b in range(n):
        where += [(full * b + j // n, j % n) for j in range(dirs - 1)] + [(full * n, b)]
    return where


def pack_kernel(n, e_hbm, c_hbm, r_hbm, *rest):
    outs, (e_ref, c_ref, r_ref, sem) = rest[:n], rest[n:]
    dirs, nfreq, npt = e_ref.shape
    copies = [
        pltpu.make_async_copy(x, y, sem.at[i])
        for i, (x, y) in enumerate(((e_hbm, e_ref), (c_hbm, c_ref), (r_hbm, r_ref)))
    ]
    for copy in copies:
        copy.start()
    for copy in copies:
        copy.wait()
    at = Spot(n, npt)
    block = at.block((nfreq, npt))
    full = (dirs - 1) // n
    last = [(at.k + a) % n for a in range(3)]
    for d in range(n):
        to = subtile_of(at.s, at.k ^ d, n)
        for a, ref in enumerate((e_ref, c_ref, r_ref)):
            for h in range(full):
                row = None
                for i in range(n):
                    piece = move(ref[n * h + i], at.shift(i, to))
                    row = piece if row is None else jnp.where(block == i, piece, row)
                outs[d][full * a + h, :nfreq, :] = row
        row = None
        for a, ref in enumerate((e_ref, c_ref, r_ref)):
            piece = move(ref[dirs - 1], at.shift(last[a], to))
            row = piece if row is None else jnp.where(block == last[a], piece, row)
        outs[d][3 * full, :nfreq, :] = row


def offset_kernel(n, nfreq, total, reach, u_ref, *refs):
    outs = refs[n:]
    dirs, npt = u_ref.shape
    at = Spot(n, npt)
    off = offsets(u_ref[...], at.s, npt, total, reach)
    block = at.block((1, npt))
    full = (dirs - 1) // n
    for d in range(n):
        to = subtile_of(at.s, at.k ^ d, n)
        turned = [move(off, at.shift(i, to)) for i in range(n)]
        for h in range(full):
            row = turned[0][n * h : n * h + 1]
            for i in range(1, n):
                row = jnp.where(block == i, turned[i][n * h + i : n * h + i + 1], row)
            outs[d][h, nfreq : nfreq + 1, :] = row
        row = move(off, at.shift(at.k, to))[dirs - 1 : dirs]
        outs[d][3 * full, nfreq : nfreq + 1, :] = row


def spread_kernel(n, g_ref, *rest):
    msgs, (pe, pc, pr, near, far) = rest[:n], rest[n:]
    rows, npt = msgs[0].shape[1:]
    nfreq = g_ref.shape[0]
    at = Spot(n, npt)
    full = (msgs[0].shape[0] - 1) // 3
    block = at.block((rows, npt))
    half = at.sub // 2
    low = lanes((rows, npt)) % at.sub < half
    for a, out in enumerate((pe, pc, pr)):
        row = None
        for d in range(n):
            b = at.k ^ d
            for h in range(full):
                out[full * b + h] = msgs[d][full * a + h]
            left = msgs[d][3 * full]
            row = left if row is None else jnp.where(block == (b + a) % n, left, row)
        out[full * n] = move(row, npt - a * at.sub) if a else row
    slabs = full * n + 1
    def fill(even):
        for out, first in ((near, not even), (far, even)):
            for g in range(slabs):
                out[g] = pe[g]
                out[slabs + g] = jnp.where(low == first, pc[g], move(pr[g], half if first else npt - half))

    pl.when(at.even)(functools.partial(fill, True))
    pl.when(jnp.logical_not(at.even))(functools.partial(fill, False))
    far[2 * slabs, :nfreq, :] = g_ref[...]
    far[2 * slabs, nfreq:, :] = jnp.zeros((rows - nfreq, npt), F32)


def window(at, own, near, far, base, nback, fback, out, where, block, turned):
    dn, df = at.shift(at.qn, at.q), at.shift(at.qf, at.q)
    dn, df = (dn + nback) % at.npt, (df + fback) % at.npt
    step = (at.qn - at.q + at.n) % at.n
    slabs = own.shape[0]
    for source, start, amount in ((near, 0, dn), (far, slabs, df)):
        for g in range(slabs):
            turned[start + g] = move(source[base + g], amount)
    for i in range(at.n):
        here, side = block == i, block == (i + step) % at.n
        for d, (g, j) in enumerate(where):
            if i == j:
                out[d] = move(jnp.where(here, own[g], jnp.where(side, turned[g], turned[slabs + g])), at.shift(at.q, i))


def hour(e, c, r, idx, out, m0s, grow1, dissip, freqs, bins, nfreq, factor):
    ndir, rows, npt = e.shape

    def moved(d):
        x = e[d]
        if factor is not None:
            x = x * factor
        index = jnp.broadcast_to(idx[pl.ds(d, 1), :], (rows, npt))
        up = jnp.take_along_axis(x, index, axis=1)
        return x + c[d] * (up - x)

    def flux(d, here, there):
        rate = r[d]
        return rate * jnp.where(rate > 0.0, here, there)

    first = moved(0)
    m0s[...] = first
    last = moved(ndir - 1)

    def body(d, carry):
        here, before, total = carry
        there = moved(d + 1)
        f = flux(d, here, there)
        turned = here - f + before
        out[d] = turned
        return there, f, total + turned

    here, before, total = lax.fori_loop(
        0, ndir - 1, body, (first, flux(ndir - 1, last, first), jnp.zeros((rows, npt), F32)), unroll=True
    )
    f = flux(ndir - 1, here, m0s[...])
    turned = here - f + before
    out[ndir - 1] = turned
    total = total + turned
    live = lax.broadcasted_iota(jnp.int32, (rows, npt), 0) < nfreq
    total = jnp.where(live, total, 0.0)
    mean = jnp.sum(total, axis=0, keepdims=True) / bins
    factor = grow1 / (1.0 + dissip * mean)
    part = jnp.where(live, factor * total, 0.0)
    zeroth = jnp.sum(part, axis=0, keepdims=True)
    first_moment = jnp.sum(part * freqs, axis=0, keepdims=True)
    return factor, 4.0 * jnp.sqrt(zeroth / bins), zeroth / first_moment


def phase_kernel(n, stage, bins, nfreq, fields_before, *refs):
    refs = list(refs)
    take = lambda count: [refs.pop(0) for _ in range(count)]
    own, far, near, table_ref = take(4)
    if stage == 0:
        pc, pr, g_ref = take(3)
    else:
        cw, rw, idx, gw = take(4)
        old = take(fields_before)
    if stage == 0:
        cw, rw, idx, gw = take(4)
    fields = take(1)[0]
    if stage < 2:
        msg = take(1)[0]
    else:
        eo = take(1)[0]
        backs = take(n - 1)
    ew, et, m0s = take(3)
    ndir, rows, npt = ew.shape
    dirs = ndir // n
    at = Spot(n, npt)
    shape = (rows, npt)
    block = at.block(shape)
    where = pieces(dirs, n)
    slabs = own.shape[0]

    def unpack(at):
        window(at, own, near, far, 0, 0, 0, ew, where, block, et)
        if stage == 0:
            half = at.sub // 2
            nback, fback = (npt - half, half) if at.even else (half, npt - half)
            window(at, pc, near, far, slabs, 0, 0, cw, where, block, et)
            window(at, pr, near, far, slabs, nback, fback, rw, where, block, et)

    at.each(unpack)
    if stage == 0:
        m0s[...] = jnp.zeros(shape, F32)
        for d in range(ndir):
            m0s[d : d + 1, :] = ew[d, nfreq : nfreq + 1, :]
        idx[...] = (lanes(shape) + m0s[...].astype(jnp.int32)) & (npt - 1)
        gw[:nfreq, :] = 1.0 + jnp.where(block[:nfreq] == at.qf, far[2 * slabs, :nfreq, :], g_ref[...])
        gw[nfreq:, :] = jnp.ones((rows - nfreq, npt), F32)
    grow1, dissip, freqs = gw[...], table_ref[0], table_ref[1]
    fa, ha, pa = hour(ew, cw, rw, idx, et, m0s, grow1, dissip, freqs, bins, nfreq, None)
    fb, hb, pb = hour(et, cw, rw, idx, ew, m0s, grow1, dissip, freqs, bins, nfreq, fa)
    if stage < 2:
        fields[...] = jnp.concatenate([ha, hb, pa, pb], axis=0)

        def pack(at):
            for g in range(slabs):
                row = None
                for d, (slab, i) in enumerate(where):
                    if slab == g:
                        piece = move(ew[d] * fb, at.shift(i, at.q))
                        row = piece if row is None else jnp.where(block == i, piece, row)
                msg[g] = row

        at.each(pack)
    else:
        h = [o[:2] for o in old] + [ha, hb]
        p = [o[2:] for o in old] + [pa, pb]
        every = jnp.concatenate(h + p + [jnp.zeros((16 - 2 * STEPS, npt), F32)], axis=0)
        fields[...] = every
        for j in range(dirs):
            eo[j] = ew[dirs * at.k + j] * fb
        m0s[...] = jnp.zeros(shape, F32)
        m0s[:16, :] = every
        tail = m0s[...]
        k = at.k

        def pack(at):
            for d in range(1, n):
                b = k ^ d
                for g in range(backs[0].shape[0]):
                    row = None
                    for i in range(n):
                        j = n * g + i
                        if j > dirs:
                            continue
                        x = ew[dirs * b + j] * fb if j < dirs else tail
                        piece = move(x, at.shift(i, at.q))
                        row = piece if row is None else jnp.where(block == i, piece, row)
                    backs[d - 1][g] = row

        at.each(pack)


def order_kernel(n, dirs, f_ref, order_ref, *rest):
    msgs, series = rest[: n - 1], rest[n - 1]
    rows, npt = f_ref.shape
    at = Spot(n, npt)
    block = at.block((rows, npt))
    fields = f_ref[...]
    for d in range(1, n):
        q = subtile_of(at.s, at.k ^ d, n)
        piece = move(msgs[d - 1][dirs // n, :rows, :], at.shift(q, dirs % n))
        fields = jnp.where(block == q, piece, fields)
    index = jnp.broadcast_to((order_ref[...] - at.s * npt).reshape(1, npt), (rows, npt))
    series[...] = jnp.take_along_axis(fields, index, axis=1)


def join_kernel(n, e_ref, *rest):
    msgs, out = rest[: n - 1], rest[n - 1]
    dirs, rows, npt = e_ref.shape
    nfreq = out.shape[1]
    at = Spot(n, npt)
    block = at.block((rows, npt))
    qs = [subtile_of(at.s, at.k ^ d, n) for d in range(1, n)]
    for j in range(dirs):
        x = e_ref[j]
        for d in range(1, n):
            piece = move(msgs[d - 1][j // n], at.shift(qs[d - 1], j % n))
            x = jnp.where(block == qs[d - 1], piece, x)
        out[j] = x[:nfreq]


def hand_kernel(tiles, own_ref, *rest):
    others, out = rest[:-1], rest[-1]
    rows, npt = out.shape
    share = npt // tiles
    s = lax.axis_index("space")
    block = lanes((16, npt)) // share
    x = own_ref[...]
    for d in range(1, tiles):
        frm = s ^ d
        piece = move(others[d - 1][...], ((frm - s + tiles) % tiles) * share)
        x = jnp.where(block == frm, piece, x)
    out[...] = x[:rows]


def call(kernel, outs, scratch, *args, hbm=0, alias=None):
    vm = pl.BlockSpec(memory_space=pltpu.VMEM)
    return pl.pallas_call(
        kernel,
        out_shape=[jax.ShapeDtypeStruct(shape, dtype) for shape, dtype in outs],
        in_specs=[pl.BlockSpec(memory_space=pltpu.HBM)] * hbm + [vm] * (len(args) - hbm),
        out_specs=[vm] * len(outs),
        scratch_shapes=scratch,
        input_output_aliases=alias or {},
        compiler_params=pltpu.CompilerParams(vmem_limit_bytes=(54600 if hbm else 40960) * 1024),
    )(*args)


def on_device(spectrum, courant, refraction, growth, dissip, upwind, send_order):
    dirs, nfreq, npt = spectrum.shape
    tiles, n = lax.axis_size("space"), lax.axis_size("spec")
    total, reach = npt * tiles, npt // 8
    ndir = dirs * n
    bins = ndir * nfreq
    full = (dirs - 1) // n
    slabs = full * n + 1
    peers = range(1, n)
    swap = lambda x, d: lax.ppermute(x, "spec", [(k, k ^ d) for k in range(n)])
    near_to = lambda x: lax.ppermute(x, ("space", "spec"), ring_route(tiles, n, False))
    far_to = lambda x: lax.ppermute(x, ("space", "spec"), ring_route(tiles, n, True))
    table = jnp.stack([dissip, frequency_table(nfreq)])
    table = jnp.broadcast_to(jnp.pad(table, ((0, 0), (0, ROWS - nfreq)))[:, :, None], (2, ROWS, npt))
    field = (ROWS, npt)
    state, packed = ((ndir, *field), F32), ((slabs, *field), F32)

    part = pltpu.VMEM(spectrum.shape, F32)
    sent = call(
        functools.partial(pack_kernel, n),
        [((3 * full + 1, *field), F32)] * n,
        [part, part, part, pltpu.SemaphoreType.DMA((3,))],
        spectrum, courant, refraction, hbm=3,
    )
    sent = call(
        functools.partial(offset_kernel, n, nfreq, total, reach),
        [((3 * full + 1, *field), F32)] * n,
        [],
        upwind, *sent, alias={1 + d: d for d in range(n)},
    )
    got = [sent[0]] + [swap(sent[d], d) for d in peers]
    e, c, r, near, far = call(
        functools.partial(spread_kernel, n),
        [packed] * 3 + [((2 * slabs, *field), F32), ((2 * slabs + 1, *field), F32)],
        [],
        growth, *got,
    )
    scratch = [pltpu.VMEM(shape, F32) for shape in ((ndir, *field), (ndir, *field), field)]
    phase = lambda stage, before, outs, *args: call(
        functools.partial(phase_kernel, n, stage, bins, nfreq, before), outs, scratch, *args
    )
    some = ((4, npt), F32)
    c, r, idx, gw, f0, e = phase(
        0, 0, [state, state, (field, jnp.int32), (field, F32), some, packed],
        e, far_to(far), near_to(near), table, c, r, growth,
    )
    f1, e = phase(1, 1, [some, packed], e, far_to(e), near_to(e), table, c, r, idx, gw, f0)
    back = ((-(-(dirs + 1) // n), *field), F32)
    fields, own, *backs = phase(
        2, 2, [((16, npt), F32), ((dirs, *field), F32)] + [back] * (n - 1),
        e, far_to(e), near_to(e), table, c, r, idx, gw, f0, f1,
    )
    backs = [swap(x, d) for d, x in zip(peers, backs)]
    (ordered,) = call(functools.partial(order_kernel, n, dirs), [((16, npt), F32)], [], fields, send_order, *backs)
    (energy,) = call(functools.partial(join_kernel, n), [(spectrum.shape, F32)], [], own, *backs)
    if tiles == 4:
        others = [lax.ppermute(ordered, "space", [(t, t ^ d) for t in range(tiles)]) for d in range(1, tiles)]
        (series,) = call(functools.partial(hand_kernel, tiles), [((2 * STEPS, npt), F32)], [], ordered, *others)
    else:
        parts = ordered[: 2 * STEPS].reshape(2 * STEPS, tiles, npt // tiles)
        series = lax.all_to_all(parts, "space", split_axis=1, concat_axis=1, tiled=True).reshape(2 * STEPS, npt)
    return (energy, series)


def solution(mesh):
    placed = (
        P("spec", None, ("runs", "space")),
        P("spec", None, "space"),
        P("spec", None, "space"),
        P(None, ("runs", "space")),
        P(),
        P("spec", "space"),
        P("space"),
    )
    return jax.shard_map(
        on_device,
        mesh=mesh,
        in_specs=placed,
        out_specs=(P("spec", None, ("runs", "space")), P(None, ("runs", "space"))),
        check_vma=False,
    )
```

```python
import functools

import jax
import jax.numpy as jnp
from jax import lax
from jax.experimental import pallas as pl
from jax.experimental.pallas import tpu as pltpu
from jax.sharding import PartitionSpec as P

STEPS = 6
ROWS = 40
F32 = jnp.float32


def frequency_table(count):
    return 0.035 * jnp.float32(1.1) ** jnp.arange(count, dtype=jnp.float32)


def orders(tiles, n):
    up = list(range(n))
    if tiles == 4 and n == 4:
        return [up, [3, 1, 0, 2], [2, 0, 1, 3], up[::-1]]
    return [up if s % 2 == 0 else up[::-1] for s in range(tiles)]


def subtile_of(s, k, n):
    tiles = lax.axis_size("space")
    table = orders(tiles, n)
    if tiles != 4:
        return jnp.where(s % 2 == 0, k, n - 1 - k)
    q = k
    for t in range(1, tiles):
        here = n - 1
        for i in range(n - 1):
            here = jnp.where(k == table[t][i], i, here)
        q = jnp.where(s == t, here, q)
    return q


def ring_route(tiles, n, far):
    table = orders(tiles, n)
    route = []
    for s in range(tiles):
        for q in range(n):
            at = s * n + q
            to = (at + (1 if (q % 2 == 0) != far else -1)) % (tiles * n)
            route.append((s * n + table[s][q], to // n * n + table[to // n][to % n]))
    return route


def lanes(shape):
    return lax.broadcasted_iota(jnp.int32, shape, len(shape) - 1)


class Spot:
    def __init__(self, n, npt, q=None):
        self.n, self.sub, self.npt = n, npt // n, npt
        if q is None:
            self.s, self.k = lax.axis_index("space"), lax.axis_index("spec")
            q = subtile_of(self.s, self.k, n)
        self.q = q
        self.qn = self.q ^ 1
        self.qf = n - 1 - self.q
        self.even = self.q % 2 == 0

    def shift(self, to, frm):
        return ((to - frm + self.n) % self.n) * self.sub

    def block(self, shape):
        return lanes(shape) // self.sub

    def each(self, body):
        for q in range(self.n):
            pl.when(self.q == q)(functools.partial(body, Spot(self.n, self.npt, q)))


def move(x, amount):
    if isinstance(amount, int) and amount == 0:
        return x
    return pltpu.roll(x, amount, 1)


def offsets(upwind, s, npt, total, reach):
    own = s * npt + lanes(upwind.shape)
    return (jnp.mod(upwind - own + reach, total) - reach).astype(F32)


def pieces(dirs, n):
    full = (dirs - 1) // n
    where = []
    for b in range(n):
        where += [(full * b + j // n, j % n) for j in range(dirs - 1)] + [(full * n, b)]
    return where


def pack_kernel(n, e_hbm, c_hbm, r_hbm, *rest):
    outs, (e_ref, c_ref, r_ref, sem) = rest[:n], rest[n:]
    dirs, nfreq, npt = e_ref.shape
    copies = [
        pltpu.make_async_copy(x, y, sem.at[i])
        for i, (x, y) in enumerate(((e_hbm, e_ref), (c_hbm, c_ref), (r_hbm, r_ref)))
    ]
    for copy in copies:
        copy.start()
    at = Spot(n, npt)
    block = at.block((nfreq, npt))
    full = (dirs - 1) // n
    last = [(at.k + a) % n for a in range(3)]
    tos = [subtile_of(at.s, at.k ^ d, n) for d in range(n)]
    for a, ref in enumerate((e_ref, c_ref, r_ref)):
        copies[a].wait()
        for d, to in enumerate(tos):
            for h in range(full):
                row = None
                for i in range(n):
                    piece = move(ref[n * h + i], at.shift(i, to))
                    row = piece if row is None else jnp.where(block == i, piece, row)
                outs[d][full * a + h, :nfreq, :] = row
    for d, to in enumerate(tos):
        row = None
        for a, ref in enumerate((e_ref, c_ref, r_ref)):
            piece = move(ref[dirs - 1], at.shift(last[a], to))
            row = piece if row is None else jnp.where(block == last[a], piece, row)
        outs[d][3 * full, :nfreq, :] = row


def offset_kernel(n, nfreq, total, reach, u_ref, *refs):
    outs = refs[n:]
    dirs, npt = u_ref.shape
    at = Spot(n, npt)
    off = offsets(u_ref[...], at.s, npt, total, reach)
    block = at.block((1, npt))
    full = (dirs - 1) // n
    for d in range(n):
        to = subtile_of(at.s, at.k ^ d, n)
        turned = [move(off, at.shift(i, to)) for i in range(n)]
        for h in range(full):
            row = turned[0][n * h : n * h + 1]
            for i in range(1, n):
                row = jnp.where(block == i, turned[i][n * h + i : n * h + i + 1], row)
            outs[d][h, nfreq : nfreq + 1, :] = row
        row = move(off, at.shift(at.k, to))[dirs - 1 : dirs]
        outs[d][3 * full, nfreq : nfreq + 1, :] = row


def spread_kernel(n, g_ref, *rest):
    msgs, (pe, pc, pr, near, far) = rest[:n], rest[n:]
    rows, npt = msgs[0].shape[1:]
    nfreq = g_ref.shape[0]
    at = Spot(n, npt)
    full = (msgs[0].shape[0] - 1) // 3
    block = at.block((rows, npt))
    half = at.sub // 2
    low = lanes((rows, npt)) % at.sub < half
    for a, out in enumerate((pe, pc, pr)):
        row = None
        for d in range(n):
            b = at.k ^ d
            for h in range(full):
                out[full * b + h] = msgs[d][full * a + h]
            left = msgs[d][3 * full]
            row = left if row is None else jnp.where(block == (b + a) % n, left, row)
        out[full * n] = move(row, npt - a * at.sub) if a else row
    slabs = full * n + 1
    def fill(even):
        for out, first in ((near, not even), (far, even)):
            for g in range(slabs):
                out[g] = pe[g]
                out[slabs + g] = jnp.where(low == first, pc[g], move(pr[g], half if first else npt - half))

    pl.when(at.even)(functools.partial(fill, True))
    pl.when(jnp.logical_not(at.even))(functools.partial(fill, False))
    far[2 * slabs, :nfreq, :] = g_ref[...]
    far[2 * slabs, nfreq:, :] = jnp.zeros((rows - nfreq, npt), F32)


def window(at, own, near, far, base, nback, fback, out, where, block, turned):
    dn, df = at.shift(at.qn, at.q), at.shift(at.qf, at.q)
    dn, df = (dn + nback) % at.npt, (df + fback) % at.npt
    step = (at.qn - at.q + at.n) % at.n
    slabs = own.shape[0]
    for source, start, amount in ((near, 0, dn), (far, slabs, df)):
        for g in range(slabs):
            turned[start + g] = move(source[base + g], amount)
    for i in range(at.n):
        here, side = block == i, block == (i + step) % at.n
        for d, (g, j) in enumerate(where):
            if i == j:
                out[d] = move(jnp.where(here, own[g], jnp.where(side, turned[g], turned[slabs + g])), at.shift(at.q, i))


def hour(e, c, r, idx, out, m0s, grow1, dissip, freqs, bins, nfreq, factor):
    ndir, rows, npt = e.shape

    def moved(d):
        x = e[d]
        if factor is not None:
            x = x * factor
        index = jnp.broadcast_to(idx[pl.ds(d, 1), :], (rows, npt))
        up = jnp.take_along_axis(x, index, axis=1)
        return x + c[d] * (up - x)

    def flux(d, here, there):
        rate = r[d]
        return rate * jnp.where(rate > 0.0, here, there)

    first = moved(0)
    m0s[...] = first
    last = moved(ndir - 1)

    def body(d, carry):
        here, before, total = carry
        there = moved(d + 1)
        f = flux(d, here, there)
        turned = here - f + before
        out[d] = turned
        return there, f, total + turned

    here, before, total = lax.fori_loop(
        0, ndir - 1, body, (first, flux(ndir - 1, last, first), jnp.zeros((rows, npt), F32)), unroll=True
    )
    f = flux(ndir - 1, here, m0s[...])
    turned = here - f + before
    out[ndir - 1] = turned
    total = total + turned
    live = lax.broadcasted_iota(jnp.int32, (rows, npt), 0) < nfreq
    total = jnp.where(live, total, 0.0)
    mean = jnp.sum(total, axis=0, keepdims=True) / bins
    factor = grow1 / (1.0 + dissip * mean)
    part = jnp.where(live, factor * total, 0.0)
    zeroth = jnp.sum(part, axis=0, keepdims=True)
    first_moment = jnp.sum(part * freqs, axis=0, keepdims=True)
    return factor, 4.0 * jnp.sqrt(zeroth / bins), zeroth / first_moment


def phase_kernel(n, stage, bins, nfreq, fields_before, *refs):
    refs = list(refs)
    take = lambda count: [refs.pop(0) for _ in range(count)]
    own, near, far, table_ref = take(4)
    if stage == 0:
        pc, pr, g_ref = take(3)
    else:
        cw, rw, idx, gw = take(4)
        old = take(fields_before)
    if stage == 0:
        cw, rw, idx, gw = take(4)
    fields = take(1)[0]
    if stage < 2:
        msg = take(1)[0]
    else:
        eo = take(1)[0]
        backs = take(n - 1)
    ew, et, m0s = take(3)
    ndir, rows, npt = ew.shape
    dirs = ndir // n
    at = Spot(n, npt)
    shape = (rows, npt)
    block = at.block(shape)
    where = pieces(dirs, n)
    slabs = own.shape[0]

    def unpack(at):
        window(at, own, near, far, 0, 0, 0, ew, where, block, et)
        if stage == 0:
            half = at.sub // 2
            nback, fback = (npt - half, half) if at.even else (half, npt - half)
            window(at, pc, near, far, slabs, 0, 0, cw, where, block, et)
            window(at, pr, near, far, slabs, nback, fback, rw, where, block, et)

    at.each(unpack)
    if stage == 0:
        m0s[...] = jnp.zeros(shape, F32)
        for d in range(ndir):
            m0s[d : d + 1, :] = ew[d, nfreq : nfreq + 1, :]
        idx[...] = (lanes(shape) + m0s[...].astype(jnp.int32)) & (npt - 1)
        gw[:nfreq, :] = 1.0 + jnp.where(block[:nfreq] == at.qf, far[2 * slabs, :nfreq, :], g_ref[...])
        gw[nfreq:, :] = jnp.ones((rows - nfreq, npt), F32)
    grow1, dissip, freqs = gw[...], table_ref[0], table_ref[1]
    fa, ha, pa = hour(ew, cw, rw, idx, et, m0s, grow1, dissip, freqs, bins, nfreq, None)
    fb, hb, pb = hour(et, cw, rw, idx, ew, m0s, grow1, dissip, freqs, bins, nfreq, fa)
    if stage < 2:
        fields[...] = jnp.concatenate([ha, hb, pa, pb], axis=0)

        def pack(at):
            for g in range(slabs):
                row = None
                for d, (slab, i) in enumerate(where):
                    if slab == g:
                        piece = move(ew[d] * fb, at.shift(i, at.q))
                        row = piece if row is None else jnp.where(block == i, piece, row)
                msg[g] = row

        at.each(pack)
    else:
        h = [o[:2] for o in old] + [ha, hb]
        p = [o[2:] for o in old] + [pa, pb]
        every = jnp.concatenate(h + p + [jnp.zeros((16 - 2 * STEPS, npt), F32)], axis=0)
        fields[...] = every
        for j in range(dirs):
            eo[j] = ew[dirs * at.k + j] * fb
        m0s[...] = jnp.zeros(shape, F32)
        m0s[:16, :] = every
        tail = m0s[...]
        k = at.k

        def pack(at):
            for d in range(1, n):
                b = k ^ d
                for g in range(backs[0].shape[0]):
                    row = None
                    for i in range(n):
                        j = n * g + i
                        if j > dirs:
                            continue
                        x = ew[dirs * b + j] * fb if j < dirs else tail
                        piece = move(x, at.shift(i, at.q))
                        row = piece if row is None else jnp.where(block == i, piece, row)
                    backs[d - 1][g] = row

        at.each(pack)


def order_kernel(n, dirs, f_ref, order_ref, *rest):
    msgs, series = rest[: n - 1], rest[n - 1]
    rows, npt = f_ref.shape
    at = Spot(n, npt)
    block = at.block((rows, npt))
    fields = f_ref[...]
    for d in range(1, n):
        q = subtile_of(at.s, at.k ^ d, n)
        piece = move(msgs[d - 1][dirs // n, :rows, :], at.shift(q, dirs % n))
        fields = jnp.where(block == q, piece, fields)
    index = jnp.broadcast_to((order_ref[...] - at.s * npt).reshape(1, npt), (rows, npt))
    series[...] = jnp.take_along_axis(fields, index, axis=1)


def join_kernel(n, e_ref, *rest):
    msgs, out = rest[: n - 1], rest[n - 1]
    dirs, rows, npt = e_ref.shape
    nfreq = out.shape[1]
    at = Spot(n, npt)
    block = at.block((rows, npt))
    qs = [subtile_of(at.s, at.k ^ d, n) for d in range(1, n)]
    for j in range(dirs):
        x = e_ref[j]
        for d in range(1, n):
            piece = move(msgs[d - 1][j // n], at.shift(qs[d - 1], j % n))
            x = jnp.where(block == qs[d - 1], piece, x)
        out[j] = x[:nfreq]


def hand_kernel(tiles, own_ref, *rest):
    others, out = rest[:-1], rest[-1]
    rows, npt = out.shape
    share = npt // tiles
    s = lax.axis_index("space")
    block = lanes((16, npt)) // share
    x = own_ref[...]
    for d in range(1, tiles):
        frm = s ^ d
        piece = move(others[d - 1][...], ((frm - s + tiles) % tiles) * share)
        x = jnp.where(block == frm, piece, x)
    out[...] = x[:rows]


def call(kernel, outs, scratch, *args, hbm=0, alias=None):
    vm = pl.BlockSpec(memory_space=pltpu.VMEM)
    return pl.pallas_call(
        kernel,
        out_shape=[jax.ShapeDtypeStruct(shape, dtype) for shape, dtype in outs],
        in_specs=[pl.BlockSpec(memory_space=pltpu.HBM)] * hbm + [vm] * (len(args) - hbm),
        out_specs=[vm] * len(outs),
        scratch_shapes=scratch,
        input_output_aliases=alias or {},
        compiler_params=pltpu.CompilerParams(vmem_limit_bytes=(54600 if hbm else 40960) * 1024),
    )(*args)


def on_device(spectrum, courant, refraction, growth, dissip, upwind, send_order):
    dirs, nfreq, npt = spectrum.shape
    tiles, n = lax.axis_size("space"), lax.axis_size("spec")
    total, reach = npt * tiles, npt // 8
    ndir = dirs * n
    bins = ndir * nfreq
    full = (dirs - 1) // n
    slabs = full * n + 1
    peers = range(1, n)
    swap = lambda x, d: lax.ppermute(x, "spec", [(k, k ^ d) for k in range(n)])
    near_to = lambda x: lax.ppermute(x, ("space", "spec"), ring_route(tiles, n, False))
    far_to = lambda x: lax.ppermute(x, ("space", "spec"), ring_route(tiles, n, True))
    table = jnp.stack([dissip, frequency_table(nfreq)])
    table = jnp.broadcast_to(jnp.pad(table, ((0, 0), (0, ROWS - nfreq)))[:, :, None], (2, ROWS, npt))
    field = (ROWS, npt)
    state, packed = ((ndir, *field), F32), ((slabs, *field), F32)

    part = pltpu.VMEM(spectrum.shape, F32)
    sent = call(
        functools.partial(pack_kernel, n),
        [((3 * full + 1, *field), F32)] * n,
        [part, part, part, pltpu.SemaphoreType.DMA((3,))],
        spectrum, courant, refraction, hbm=3,
    )
    sent = call(
        functools.partial(offset_kernel, n, nfreq, total, reach),
        [((3 * full + 1, *field), F32)] * n,
        [],
        upwind, *sent, alias={1 + d: d for d in range(n)},
    )
    got = [sent[0]] + [swap(sent[d], d) for d in peers]
    e, c, r, near, far = call(
        functools.partial(spread_kernel, n),
        [packed] * 3 + [((2 * slabs, *field), F32), ((2 * slabs + 1, *field), F32)],
        [],
        growth, *got,
    )
    scratch = [pltpu.VMEM(shape, F32) for shape in ((ndir, *field), (ndir, *field), field)]
    phase = lambda stage, before, outs, *args: call(
        functools.partial(phase_kernel, n, stage, bins, nfreq, before), outs, scratch, *args
    )
    some = ((4, npt), F32)
    c, r, idx, gw, f0, e = phase(
        0, 0, [state, state, (field, jnp.int32), (field, F32), some, packed],
        e, near_to(near), far_to(far), table, c, r, growth,
    )
    f1, e = phase(1, 1, [some, packed], e, near_to(e), far_to(e), table, c, r, idx, gw, f0)
    back = ((-(-(dirs + 1) // n), *field), F32)
    fields, own, *backs = phase(
        2, 2, [((16, npt), F32), ((dirs, *field), F32)] + [back] * (n - 1),
        e, near_to(e), far_to(e), table, c, r, idx, gw, f0, f1,
    )
    backs = [swap(x, d) for d, x in zip(peers, backs)]
    (ordered,) = call(functools.partial(order_kernel, n, dirs), [((16, npt), F32)], [], fields, send_order, *backs)
    (energy,) = call(functools.partial(join_kernel, n), [(spectrum.shape, F32)], [], own, *backs)
    if tiles == 4:
        others = [lax.ppermute(ordered, "space", [(t, t ^ d) for t in range(tiles)]) for d in range(1, tiles)]
        (series,) = call(functools.partial(hand_kernel, tiles), [((2 * STEPS, npt), F32)], [], ordered, *others)
    else:
        parts = ordered[: 2 * STEPS].reshape(2 * STEPS, tiles, npt // tiles)
        series = lax.all_to_all(parts, "space", split_axis=1, concat_axis=1, tiled=True).reshape(2 * STEPS, npt)
    return (energy, series)


def solution(mesh):
    placed = (
        P("spec", None, ("runs", "space")),
        P("spec", None, "space"),
        P("spec", None, "space"),
        P(None, ("runs", "space")),
        P(),
        P("spec", "space"),
        P("space"),
    )
    return jax.shard_map(
        on_device,
        mesh=mesh,
        in_specs=placed,
        out_specs=(P("spec", None, ("runs", "space")), P(None, ("runs", "space"))),
        check_vma=False,
    )
```
